256 devices in a mesh: angle: 8 (over x_hi, y), batch: 32 (over z, x_lo, core).
Axes of the slice: x: 4 (x_hi: 2, x_lo: 2; x = x_hi * 2 + x_lo), y: 4, z: 8, core: 2. Of those that a mesh axis runs over, the one named last changes fastest.
Arguments:
- signals: bfloat16 [32, 24576, 256], P('batch', 'angle'), may hold values from -6 to 6
- cotangent: bfloat16 [32, 24576, 256], P('batch', 'angle'), may hold values from -6 to 6
- first_dilated_kernel: bfloat16 [3, 256, 256], replicated, may hold values from -0.21875 to 0.21875
- first_conv_bias: float32 [256], replicated, may hold values from -3 to 3
- first_output_projection: bfloat16 [256, 256], replicated, may hold values from -0.375 to 0.375
- second_dilated_kernel: bfloat16 [3, 256, 256], replicated, may hold values from -0.21875 to 0.21875
- second_conv_bias: float32 [256], replicated, may hold values from -3 to 3
- second_output_projection: bfloat16 [256, 256], replicated, may hold values from -0.375 to 0.375
Outputs:
- signal_input_gradient: bfloat16 [32, 24576, 256], P('batch', 'angle')
- conv_grad_a: float32 [3, 256, 256], replicated
- bias_grad_a: float32 [256], replicated
- proj_grad_a: float32 [256, 256], replicated
- conv_grad_b: float32 [3, 256, 256], replicated
- bias_grad_b: float32 [256], replicated
- proj_grad_b: float32 [256, 256], replicated
The draws below stay inside these ranges and needn't reach their ends.
All inputs are finite; a program needn't handle non-finite values.
Results may differ from the reference program's by a relative error of at most 0.013.
Values may be sent and summed in bfloat16 or wider, within the bound.
No kernel may reach another device: no remote copies, remote signals or barrier semaphores. Data moves between devices by JAX's collectives and lax.ppermute only.
A program may use at most 64 MiB of HBM per device.

```python
import math
import jax
import jax.numpy as jnp
from jax import lax

C = 256
FIRST_DILATION = 512
SECOND_DILATION = 1024
LENGTH = 24576
TURBINES = 32


def steps_of(stream_key, dims, split, low, largest):
    factor_of = 1.0
    for dim, blocks in split:
        steps = jax.random.uniform(jax.random.fold_in(jax.random.fold_in(stream_key, 6), dim), (blocks,), jnp.float32, low / len(split), largest / len(split))
        factor_of = factor_of * jnp.repeat(jnp.exp(steps), dims[dim] // blocks).reshape((-1,) + (1,) * (len(dims) - 1 - dim))
    return factor_of


def normal_values(own_key, extent, width, reach, split=(), dtype=jnp.bfloat16):
    drawn = jax.random.normal(own_key, extent, jnp.float32) * width
    if len(split) > 0:
        drawn = steps_of(own_key, extent, split, -0.22, 0.18) * drawn
    return jnp.clip(drawn, min=-reach, max=reach).astype(dtype)


def setup_inputs(seed: int = 0) -> dict:
    key_list = jax.random.split(jax.random.key(seed), 9)
    return {
        "signals": normal_values(key_list[0], (TURBINES, LENGTH, C), 1.0, 6.0, ((0, 32), (1, 8))),
        "cotangent": normal_values(key_list[1], (TURBINES, LENGTH, C), 1.0, 6.0, ((0, 32), (1, 8))),
        "first_dilated_kernel": normal_values(key_list[2], (3, C, C), (3 * C) ** -0.5, 0.21875),
        "first_conv_bias": normal_values(key_list[3], (C,), 0.5, 3.0, (), jnp.float32),
        "first_output_projection": normal_values(key_list[4], (C, C), C ** -0.5, 0.375),
        "second_dilated_kernel": normal_values(key_list[5], (3, C, C), (3 * C) ** -0.5, 0.21875),
        "second_conv_bias": normal_values(key_list[6], (C,), 0.5, 3.0, (), jnp.float32),
        "second_output_projection": normal_values(key_list[7], (C, C), C ** -0.5, 0.375),
    }


def gelu_exact(v):
    return 0.5 * v * (1.0 + lax.erf(v / math.sqrt(2.0)))

def gelu_slope(v):
    return 0.5 * (1.0 + lax.erf(v / math.sqrt(2.0))) + v * jnp.exp(-0.5 * v * v) / math.sqrt(2.0 * math.pi)

def kernel_taps_count(field, kernel, dilation):
    total = jnp.zeros((field.shape[0], kernel.shape[2]), jnp.float32)
    for k in range(3):
        total = total + jnp.dot(jnp.roll(field, -(k - 1) * dilation, 0), kernel[k], preferred_element_type=jnp.float32)
    return total

def residual_block_backward(field, upstream, act, pre, kernel, proj, dilation):
    proj_grad = jnp.dot(act.T, upstream, preferred_element_type=jnp.float32)
    delta = (jnp.dot(upstream, proj.T, preferred_element_type=jnp.float32) * gelu_slope(pre)).astype(jnp.bfloat16)
    bias_grad = lax.optimization_barrier(jnp.sum(delta.astype(jnp.float32), axis=0))
    conv_grad = jnp.stack([jnp.dot(jnp.roll(field, -(k - 1) * dilation, 0).T, delta, preferred_element_type=jnp.float32) for k in range(3)])
    below = upstream.astype(jnp.float32)
    for k in range(3):
        below = below + jnp.dot(jnp.roll(delta, (k - 1) * dilation, 0), kernel[k].T, preferred_element_type=jnp.float32)
    return (below.astype(jnp.bfloat16), conv_grad, bias_grad, proj_grad)

def one_signal(pair, first_dilated_kernel, first_conv_bias, first_output_projection, second_dilated_kernel, second_conv_bias, second_output_projection):
    vibration_input, cotangent = pair
    first_preactivation = kernel_taps_count(vibration_input, first_dilated_kernel, FIRST_DILATION) + first_conv_bias
    first_activation = gelu_exact(first_preactivation).astype(jnp.bfloat16)
    between_blocks = (vibration_input.astype(jnp.float32) + jnp.dot(first_activation, first_output_projection, preferred_element_type=jnp.float32)).astype(jnp.bfloat16)
    second_preactivation = kernel_taps_count(between_blocks, second_dilated_kernel, SECOND_DILATION) + second_conv_bias
    second_activation = gelu_exact(second_preactivation).astype(jnp.bfloat16)
    between_blocks_gradient, second_kernel_gradient, second_bias_gradient, second_projection_gradient = residual_block_backward(between_blocks, cotangent, second_activation, second_preactivation, second_dilated_kernel, second_output_projection, SECOND_DILATION)
    signal_input_gradient, first_kernel_gradient, first_bias_gradient, first_projection_gradient = residual_block_backward(vibration_input, between_blocks_gradient, first_activation, first_preactivation, first_dilated_kernel, first_output_projection, FIRST_DILATION)
    return (signal_input_gradient, first_kernel_gradient, first_bias_gradient, first_projection_gradient, second_kernel_gradient, second_bias_gradient, second_projection_gradient)

def reference(signals, cotangent, first_dilated_kernel, first_conv_bias, first_output_projection, second_dilated_kernel, second_conv_bias, second_output_projection):
    results = lax.map(lambda pair: one_signal(pair, first_dilated_kernel, first_conv_bias, first_output_projection, second_dilated_kernel, second_conv_bias, second_output_projection), (signals, cotangent))
    signal_input_gradient = results[0]
    sums = [lax.optimization_barrier(jnp.sum(item, axis=0)) for item in results[1:]]
    return (signal_input_gradient, sums[0], sums[1], sums[2], sums[3], sums[4], sums[5])
```

```python
import math

import jax
import jax.numpy as jnp
from jax import lax
from jax.sharding import PartitionSpec as P

FIRST_DILATION = 512
SECOND_DILATION = 1024


def extended(cells, sides, width):
    for axis, dim in sides:
        count = lax.axis_size(axis)
        head = lax.slice_in_dim(cells, 0, width, axis=dim)
        tail = lax.slice_in_dim(cells, cells.shape[dim] - width, cells.shape[dim], axis=dim)
        cells = jnp.concatenate(
            [
                lax.ppermute(tail, axis, [(i, (i + 1) % count) for i in range(count)]),
                cells,
                lax.ppermute(head, axis, [((i + 1) % count, i) for i in range(count)]),
            ],
            axis=dim,
        )
    return cells


def gelu_exact(v):
    return 0.5 * v * (1.0 + lax.erf(v / math.sqrt(2.0)))


def gelu_slope(v):
    return 0.5 * (1.0 + lax.erf(v / math.sqrt(2.0))) + v * jnp.exp(-0.5 * v * v) / math.sqrt(
        2.0 * math.pi
    )


def wrap_extended(field, dilation):
    return extended(field, (("angle", 1),), dilation)


def dilated_forward(padded, kernel, bias, dilation, sequence_length):
    total = jnp.zeros(padded.shape[:1] + (sequence_length, kernel.shape[2]), jnp.float32)
    for k in range(3):
        window = padded[:, k * dilation : k * dilation + sequence_length]
        total = total + jnp.einsum(
            "btc,cd->btd", window, kernel[k], preferred_element_type=jnp.float32
        )
    return total + bias


def reduce_grads(matrices, biases):
    angles, turbines = lax.axis_size("angle"), lax.axis_size("batch")
    parts, rows, lanes = matrices.shape
    share = biases.size // parts
    extra = jnp.pad(biases.reshape(parts, 1, share), ((0, 0), (0, 7), (0, lanes - share)))
    sent = jnp.concatenate([matrices, extra], axis=1).astype(jnp.bfloat16)
    got = lax.all_to_all(sent, "angle", 0, 0)
    total = jnp.sum(got.astype(jnp.float32), axis=0)
    small = share // turbines
    sent = jnp.concatenate(
        [
            total[:rows].reshape(turbines, rows // turbines, lanes),
            jnp.pad(
                total[rows, :share].reshape(turbines, 1, small),
                ((0, 0), (0, rows // turbines - 1), (0, 128 - small)),
            ),
        ],
        axis=2,
    ).astype(jnp.bfloat16)
    got = lax.all_to_all(sent, "batch", 0, 0)
    total = jnp.sum(got.astype(jnp.float32), axis=0).astype(jnp.bfloat16)
    got = lax.all_to_all(jnp.broadcast_to(total, (turbines,) + total.shape), "batch", 0, 0)
    matrix = got[:, :, :lanes].reshape(rows, lanes)
    bias = jnp.pad(got[:, 0, lanes : lanes + small].reshape(1, share), ((0, 7), (0, lanes - share)))
    own = jnp.concatenate([matrix, bias], axis=0)
    got = lax.all_to_all(jnp.broadcast_to(own, (angles,) + own.shape), "angle", 0, 0)
    got = got.astype(jnp.float32)
    return got[:, :rows], got[:, rows, :share].reshape(biases.shape)


def lower_grad(delta, upstream, kernel, dilation, sequence_length):
    below = upstream.astype(jnp.float32)
    padded = extended(delta, (("angle", 1),), dilation)
    for k in range(3):
        window = padded[:, (2 - k) * dilation : (2 - k) * dilation + sequence_length]
        below = below + jnp.einsum(
            "btd,cd->btc", window, kernel[k], preferred_element_type=jnp.float32
        )
    return below.astype(jnp.bfloat16)


def residual_block_backward(padded, upstream, act, pre, kernel, proj, dilation, sequence_length):
    proj_grad = jnp.einsum("btc,btd->cd", act, upstream, preferred_element_type=jnp.float32)
    delta = (
        jnp.einsum("btd,cd->btc", upstream, proj, preferred_element_type=jnp.float32)
        * gelu_slope(pre)
    ).astype(jnp.bfloat16)
    bias_grad = jnp.sum(delta.astype(jnp.float32), axis=(0, 1))
    conv_grad = jnp.stack(
        [
            jnp.einsum(
                "btc,btd->cd",
                padded[:, k * dilation : k * dilation + sequence_length],
                delta,
                preferred_element_type=jnp.float32,
            )
            for k in range(3)
        ]
    )
    below = lower_grad(delta, upstream, kernel, dilation, sequence_length)
    return (below, (conv_grad, bias_grad, proj_grad))


def on_device(
    signals,
    cotangent,
    first_dilated_kernel,
    first_conv_bias,
    first_output_projection,
    second_dilated_kernel,
    second_conv_bias,
    second_output_projection,
):
    sequence_length = signals.shape[1]
    first_padded_input = wrap_extended(signals, FIRST_DILATION)
    first_preactivation = dilated_forward(
        first_padded_input, first_dilated_kernel, first_conv_bias, FIRST_DILATION, sequence_length
    )
    first_activation = gelu_exact(first_preactivation).astype(jnp.bfloat16)
    between_blocks = (
        signals.astype(jnp.float32)
        + jnp.einsum(
            "btc,cd->btd",
            first_activation,
            first_output_projection,
            preferred_element_type=jnp.float32,
        )
    ).astype(jnp.bfloat16)
    second_padded_input = wrap_extended(between_blocks, SECOND_DILATION)
    second_preactivation = dilated_forward(
        second_padded_input,
        second_dilated_kernel,
        second_conv_bias,
        SECOND_DILATION,
        sequence_length,
    )
    second_activation = gelu_exact(second_preactivation).astype(jnp.bfloat16)
    between_blocks_gradient, grads_b = residual_block_backward(
        second_padded_input,
        cotangent,
        second_activation,
        second_preactivation,
        second_dilated_kernel,
        second_output_projection,
        SECOND_DILATION,
        sequence_length,
    )
    signal_input_gradient, grads_a = residual_block_backward(
        first_padded_input,
        between_blocks_gradient,
        first_activation,
        first_preactivation,
        first_dilated_kernel,
        first_output_projection,
        FIRST_DILATION,
        sequence_length,
    )
    matrices, biases = reduce_grads(
        jnp.concatenate([grads_b[0], grads_b[2][None], grads_a[0], grads_a[2][None]]),
        jnp.stack([grads_b[1], grads_a[1]]),
    )
    return (
        signal_input_gradient,
        matrices[4:7],
        biases[1],
        matrices[7],
        matrices[0:3],
        biases[0],
        matrices[3],
    )


def solution(mesh):
    in_specs = (P("batch", "angle", None), P("batch", "angle", None), P(), P(), P(), P(), P(), P())
    out_specs = (P("batch", "angle", None), P(), P(), P(), P(), P(), P())
    return jax.shard_map(
        on_device, mesh=mesh, in_specs=in_specs, out_specs=out_specs, check_vma=False
    )
```

```python
import math

import jax
import jax.numpy as jnp
from jax import lax
from jax.experimental import pallas as pl
from jax.experimental.pallas import tpu as pltpu
from jax.sharding import Mesh, PartitionSpec as P

BLOCK = 512
RING = ("xh", "y")
REST = ("z", "xl")
BF, F32 = jnp.bfloat16, jnp.float32
C = 256


def dot(a, b):
    return jnp.dot(a, b, preferred_element_type=F32)


def t_dot(a, b):
    return lax.dot_general(a, b, (((0,), (0,)), ((), ())), preferred_element_type=F32)


def normal_cdf(v):
    return 0.5 * (1.0 + lax.erf(v * math.sqrt(0.5)))


def slope_of(v, cdf):
    return cdf + v * jnp.exp(-0.5 * v * v) * (1.0 / math.sqrt(2.0 * math.pi))


def taps(at, j, hop):
    return jnp.concatenate([at(j - hop), at(j), at(j + hop)], axis=1)


def cut_kernel(s_ref, left_ref, right_ref, sems):
    n = s_ref.shape[0]
    one = pltpu.make_async_copy(s_ref.at[pl.ds(0, 3)], left_ref, sems.at[0])
    two = pltpu.make_async_copy(s_ref.at[pl.ds(n - 3, 3)], right_ref, sems.at[1])
    one.start()
    two.start()
    one.wait()
    two.wait()


def near_kernel(
    s_ref, w_ref, bias_ref, proj_ref, w2_ref, proj2_ref,
    act_ref, slope_ref, mid_ref, w_t_ref, w2_t_ref, proj_t_ref, proj2_t_ref,
):
    at = lambda j: s_ref[j]

    def product(j):
        return dot(taps(at, j, 1), w_ref[...]) + bias_ref[...]

    pre = product(1)
    for j in range(1, 5):
        after = product(j + 1) if j < 4 else None
        cdf = normal_cdf(pre)
        act = (pre * cdf).astype(BF)
        act_ref[j - 1] = act
        slope_ref[j - 1] = slope_of(pre, cdf).astype(BF)
        mid_ref[j - 1] = (s_ref[j].astype(F32) + dot(act, proj_ref[...])).astype(BF)
        pre = after
    for k in range(3):
        to = slice((2 - k) * C, (3 - k) * C)
        w_t_ref[to] = w_ref[k * C : (k + 1) * C].T
        w2_t_ref[to] = w2_ref[k * C : (k + 1) * C].T
    proj_t_ref[...] = proj_ref[...].T
    proj2_t_ref[...] = proj2_ref[...].T


def far_kernel(
    s_ref, left_ref, right_ref, up_ref, near_ref, w_ref, bias_ref, proj_ref, w2_ref, bias2_ref, proj2_ref,
    act_ref, slope_ref, mid_ref, act2_ref, delta_ref, to_left_ref, to_right_ref,
):
    def at(j):
        return left_ref[j + 3] if j < 0 else right_ref[j - 6] if j > 5 else s_ref[j]

    def mid_at(j):
        return mid_ref[j + 2] if j < 1 else mid_ref[j - 2] if j > 4 else near_ref[j - 1]

    def product(j):
        return dot(taps(at, j, 1), w_ref[...]) + bias_ref[...]

    def product2(j):
        return dot(taps(mid_at, j, 2), w2_ref[...]) + bias2_ref[...]

    order = (0, 5, -2, 7, -1, 6)
    order2 = (2, 3, 0, 5, 1, 4)
    pre = product(order[0])
    for i, j in enumerate(order):
        after = product(order[i + 1]) if i < 5 else product2(order2[0])
        cdf = normal_cdf(pre)
        act = (pre * cdf).astype(BF)
        if j in (0, 5):
            act_ref[j // 5] = act
            slope_ref[j // 5] = slope_of(pre, cdf).astype(BF)
        mid = (at(j).astype(F32) + dot(act, proj_ref[...])).astype(BF)
        mid_ref[j + 2 if j < 1 else j - 2] = mid
        pre = after
    for i, j in enumerate(order2):
        back = dot(up_ref[j], proj2_ref[...])
        after = product2(order2[i + 1]) if i < 5 else None
        cdf = normal_cdf(pre)
        act2_ref[j] = (pre * cdf).astype(BF)
        delta = (back * slope_of(pre, cdf)).astype(BF)
        delta_ref[j] = delta
        if j < 2:
            to_left_ref[j] = delta
        if j > 3:
            to_right_ref[j - 4] = delta
        pre = after


def add_grads(sum_ref, j, cells, delta, act, up):
    conv = t_dot(cells, delta)
    proj = t_dot(act, up)
    if j == 0:
        sum_ref[: 3 * C] = conv
        sum_ref[3 * C :] = proj
    else:
        sum_ref[: 3 * C] += conv
        sum_ref[3 * C :] += proj


def put_halves(sum_ref, base, away_ref, mine_ref):
    core = lax.axis_index("core")
    half = 2 * C
    to = slice(base, base + half)
    mine_ref[to] = sum_ref[pl.ds(pl.multiple_of(core * half, half), half)].astype(BF)
    away_ref[to] = sum_ref[pl.ds(pl.multiple_of((1 - core) * half, half), half)].astype(BF)


def grads_b_kernel(near_ref, far_ref, act_ref, up_ref, delta_ref, sum_ref, bias_ref):
    def mid_at(j):
        return far_ref[j + 2] if j < 1 else far_ref[j - 2] if j > 4 else near_ref[j - 1]

    bias = jnp.zeros((1, C), F32)
    for j in range(6):
        delta = delta_ref[j]
        add_grads(sum_ref, j, taps(mid_at, j, 2), delta, act_ref[j], up_ref[j])
        bias += jnp.sum(delta.astype(F32), axis=0, keepdims=True)
    bias_ref[...] = bias


def lower_b_kernel(
    delta_ref, left_ref, right_ref, up_ref, w_ref, proj_ref, slope_ref, slope_far_ref,
    grad_ref, out_ref, to_left_ref, to_right_ref,
):
    def at(j):
        return left_ref[j + 2] if j < 0 else right_ref[j - 6] if j > 5 else delta_ref[j]

    def product(j):
        return (up_ref[j].astype(F32) + dot(taps(at, j, 2), w_ref[...])).astype(BF)

    order = (0, 5, 1, 4, 2, 3)
    below = product(order[0])
    for i, j in enumerate(order):
        after = product(order[i + 1]) if i < 5 else None
        grad_ref[j] = below
        slope = slope_far_ref[j // 5] if j in (0, 5) else slope_ref[j - 1]
        delta = (dot(below, proj_ref[...]) * slope.astype(F32)).astype(BF)
        out_ref[j] = delta
        if j == 0:
            to_left_ref[0] = delta
        if j == 5:
            to_right_ref[0] = delta
        below = after


def grads_a_kernel(
    s_ref, left_ref, right_ref, act_ref, act_far_ref, up_ref, delta_ref, other_ref, other_bias_ref,
    away_ref, mine_ref, sum_ref,
):
    def at(j):
        return left_ref[2] if j < 0 else right_ref[0] if j > 5 else s_ref[j]

    bias = jnp.zeros((1, C), F32)
    for j in range(6):
        delta = delta_ref[j]
        act = act_far_ref[j // 5] if j in (0, 5) else act_ref[j - 1]
        add_grads(sum_ref, j, taps(at, j, 1), delta, act, up_ref[j])
        bias += jnp.sum(delta.astype(F32), axis=0, keepdims=True)
    put_halves(other_ref, 0, away_ref, mine_ref)
    put_halves(sum_ref, 2 * C, away_ref, mine_ref)
    row = lax.broadcasted_iota(jnp.int32, (16, C), 0)
    tail = jnp.where(row == 0, jnp.broadcast_to(other_bias_ref[...], (16, C)), 0.0)
    tail = jnp.where(row == 1, jnp.broadcast_to(bias, (16, C)), tail).astype(BF)
    mine_ref[4 * C :] = tail
    away_ref[4 * C :] = tail


def pair_kernel(mine_ref, near_ref, out_ref):
    n, rows, _ = out_ref.shape
    chunk = (rows - 16) // 2
    tail = (mine_ref[4 * C :].astype(F32) + near_ref[4 * C :].astype(F32)).astype(BF)
    for i in range(n):
        for base, to in ((0, 0), (2 * C, chunk)):
            part = slice(base + i * chunk, base + (i + 1) * chunk)
            total = mine_ref[part].astype(F32) + near_ref[part].astype(F32)
            out_ref[i, to : to + chunk] = total.astype(BF)
        out_ref[i, 2 * chunk :] = tail


def rest_kernel(got_ref, left_ref, right_ref, out_ref):
    total = jnp.sum(got_ref[...].astype(F32), axis=0).astype(BF)
    for i in range(out_ref.shape[0]):
        out_ref[i] = total


def ring_kernel(got_ref, out_ref, bias_b_ref, bias_a_ref):
    total = jnp.sum(got_ref[...].astype(F32), axis=0)
    chunk = out_ref.shape[1]
    own = total[:chunk].astype(BF)
    for i in range(out_ref.shape[0]):
        out_ref[i] = own
    bias_b_ref[...] = total[chunk : chunk + 1]
    bias_a_ref[...] = total[chunk + 1 : chunk + 2]


def tail_kernel(mine_ref, other_ref, conv_b_ref, proj_b_ref, conv_a_ref, proj_a_ref):
    core = lax.axis_index("core")
    n, rows, _ = mine_ref.shape
    chunk = rows // 2

    def put(low, high):
        for i in range(n // 2):
            to = slice(i * chunk, (i + 1) * chunk)
            for part, conv, proj in ((0, conv_b_ref, proj_b_ref), (1, conv_a_ref, proj_a_ref)):
                of = slice(part * chunk, (part + 1) * chunk)
                conv[0, to] = low[i, of].astype(F32)
                conv[1, to] = low[i + n // 2, of].astype(F32)
                conv[2, to] = high[i, of].astype(F32)
                proj[to] = high[i + n // 2, of].astype(F32)

    @pl.when(core == 0)
    def _():
        put(mine_ref, other_ref)

    @pl.when(core != 0)
    def _():
        put(other_ref, mine_ref)


def lower_a_kernel(delta_ref, left_ref, right_ref, up_ref, w_ref, out_ref):
    def at(j):
        return left_ref[0] if j < 0 else right_ref[0] if j > 5 else delta_ref[j]

    for j in (1, 2, 3, 4, 0, 5):
        below = up_ref[j].astype(F32) + dot(taps(at, j, 1), w_ref[...])
        out_ref[j] = below.astype(BF)


def call(kernel, outs, args, flops=0, scratch=(), loose=0):
    vmem = pl.BlockSpec(memory_space=pltpu.VMEM)
    moved = sum(a.size * a.dtype.itemsize for a in args) + sum(
        math.prod(s) * jnp.dtype(t).itemsize for s, t in outs
    )
    return pl.pallas_call(
        kernel,
        out_shape=[jax.ShapeDtypeStruct(s, t) for s, t in outs],
        in_specs=[vmem] * (len(args) - loose) + [pl.BlockSpec(memory_space=pl.ANY)] * loose,
        out_specs=[vmem] * len(outs),
        scratch_shapes=list(scratch),
        compiler_params=pltpu.CompilerParams(vmem_limit_bytes=32 * 2**20),
        cost_estimate=pl.CostEstimate(flops=flops, bytes_accessed=moved, transcendentals=0),
        name=kernel.__name__[: -len("_kernel")],
    )(*args)


def from_left(cells):
    n = lax.axis_size(RING)
    return lax.ppermute(cells, RING, [(i, (i + 1) % n) for i in range(n)])


def from_right(cells):
    n = lax.axis_size(RING)
    return lax.ppermute(cells, RING, [((i + 1) % n, i) for i in range(n)])


def across(cells):
    return lax.ppermute(cells, "core", [(0, 1), (1, 0)])


def on_device(signals, cotangent, kernel_a, bias_a, proj_a, kernel_b, bias_b, proj_b):
    batch, length, channels = signals.shape
    unit = 2 * BLOCK * C * C
    cells = signals.reshape(-1, BLOCK, C)
    up = cotangent.reshape(-1, BLOCK, C)
    rest, ring = lax.axis_size(REST), lax.axis_size(RING)
    wa, wb = kernel_a.reshape(3 * C, C), kernel_b.reshape(3 * C, C)
    ba, bb = bias_a.reshape(1, C), bias_b.reshape(1, C)

    def like(n):
        return ((n, BLOCK, C), BF)

    to_left, to_right = call(
        cut_kernel, [like(3)] * 2, [cells], scratch=[pltpu.SemaphoreType.DMA((2,))], loose=1
    )
    s_left, s_right = from_left(to_right), from_right(to_left)
    act_near, slope_near, mid_near, wa_t, wb_t, pa_t, pb_t = call(
        near_kernel,
        [like(4)] * 3 + [((3 * C, C), BF)] * 2 + [((C, C), BF)] * 2,
        [cells, wa, ba, proj_a, wb, proj_b],
        16 * unit,
    )
    act_far, slope_far, mid_far, act_b, delta_b, to_left, to_right = call(
        far_kernel,
        [like(2), like(2), like(6), like(6), like(6), like(2), like(2)],
        [cells, s_left, s_right, up, mid_near, wa, ba, proj_a, wb, bb, pb_t],
        48 * unit,
    )
    d_left, d_right = from_left(to_right), from_right(to_left)
    sum_b, part_bias_b = call(
        grads_b_kernel,
        [((4 * C, C), F32), ((1, C), F32)],
        [mid_near, mid_far, act_b, up, delta_b],
        24 * unit,
    )
    grad, delta_a, to_left, to_right = call(
        lower_b_kernel,
        [like(6), like(6), like(1), like(1)],
        [delta_b, d_left, d_right, up, wb_t, pa_t, slope_near, slope_far],
        24 * unit,
    )
    e_left, e_right = from_left(to_right), from_right(to_left)
    away, mine = call(
        grads_a_kernel,
        [((4 * C + 16, C), BF)] * 2,
        [cells, s_left, s_right, act_near, act_far, grad, delta_a, sum_b, part_bias_b],
        24 * unit,
        [pltpu.VMEM((4 * C, C), F32)],
    )
    chunk = 2 * C // rest
    (sent,) = call(pair_kernel, [((rest, 2 * chunk + 16, C), BF)], [mine, across(away)])
    got = lax.all_to_all(sent, REST, 0, 0)
    (sent,) = call(
        rest_kernel, [((ring, 2 * chunk + 16, C), BF)], [got, e_left, e_right], loose=2
    )
    got = lax.all_to_all(sent, RING, 0, 0)
    sent, sum_bias_b, sum_bias_a = call(
        ring_kernel, [((rest, 2 * chunk, C), BF), ((1, C), F32), ((1, C), F32)], [got]
    )
    mine = lax.all_to_all(sent, REST, 0, 0)
    conv_b, grad_proj_b, conv_a, grad_proj_a = call(
        tail_kernel, [((3, C, C), F32), ((C, C), F32)] * 2, [mine, across(mine)]
    )
    (out,) = call(lower_a_kernel, [like(6)], [delta_a, e_left, e_right, grad, wa_t], 18 * unit)
    return (
        out.reshape(batch, length, channels),
        conv_a,
        sum_bias_a.reshape(C),
        grad_proj_a,
        conv_b,
        sum_bias_b.reshape(C),
        grad_proj_b,
    )


def solution(mesh):
    split = Mesh(mesh.devices.reshape(2, 4, 8, 2, 2), RING + REST + ("core",))
    data = P(REST + ("core",), RING, None)
    return jax.shard_map(
        on_device,
        mesh=split,
        in_specs=(data, data, P(), P(), P(), P(), P(), P()),
        out_specs=(data, P(), P(), P(), P(), P(), P()),
        check_vma=False,
    )
```

```python
import math

import jax
import jax.numpy as jnp
from jax import lax
from jax.experimental import pallas as pl
from jax.experimental.pallas import tpu as pltpu
from jax.sharding import Mesh, PartitionSpec as P

BLOCK = 512
RING = ("xh", "y")
PLANE = ("xh", "y", "xl")
COLUMN = "z"
BF, F32 = jnp.bfloat16, jnp.float32
C = 256


def dot(a, b):
    return jnp.dot(a, b, preferred_element_type=F32)


def t_dot(a, b):
    return lax.dot_general(a, b, (((0,), (0,)), ((), ())), preferred_element_type=F32)


def normal_cdf(v):
    return 0.5 * (1.0 + lax.erf(v * math.sqrt(0.5)))


def slope_of(v, cdf):
    return cdf + v * jnp.exp(-0.5 * v * v) * (1.0 / math.sqrt(2.0 * math.pi))


def taps(at, j, hop):
    return jnp.concatenate([at(j - hop), at(j), at(j + hop)], axis=1)


def cut_kernel(s_ref, left_ref, right_ref, sems):
    n = s_ref.shape[0]
    one = pltpu.make_async_copy(s_ref.at[pl.ds(0, 3)], left_ref, sems.at[0])
    two = pltpu.make_async_copy(s_ref.at[pl.ds(n - 3, 3)], right_ref, sems.at[1])
    one.start()
    two.start()
    one.wait()
    two.wait()


def tap(w_ref, k):
    return w_ref[k * C : (k + 1) * C]


def near_kernel(
    s_ref, up_ref, w_ref, bias_ref, proj_ref, w2_ref, bias2_ref, proj2_ref,
    act_ref, slope_ref, mid_ref, pre_ref, pre2_ref, back_ref, w_t_ref, w2_t_ref, proj_t_ref,
):
    at = lambda j: s_ref[j]

    def product(j):
        return dot(taps(at, j, 1), w_ref[...]) + bias_ref[...]

    pre = product(1)
    for j in range(1, 5):
        after = product(j + 1) if j < 4 else None
        cdf = normal_cdf(pre)
        act = (pre * cdf).astype(BF)
        act_ref[j - 1] = act
        slope_ref[j - 1] = slope_of(pre, cdf).astype(BF)
        mid_ref[j - 1] = (s_ref[j].astype(F32) + dot(act, proj_ref[...])).astype(BF)
        pre = after
    pre_ref[0] = dot(s_ref[0], tap(w_ref, 2)) + bias_ref[...]
    pre_ref[1] = dot(s_ref[0], tap(w_ref, 1)) + dot(s_ref[1], tap(w_ref, 2)) + bias_ref[...]
    pre_ref[2] = dot(s_ref[4], tap(w_ref, 0)) + dot(s_ref[5], tap(w_ref, 1)) + bias_ref[...]
    pre_ref[3] = dot(s_ref[5], tap(w_ref, 0)) + bias_ref[...]
    for j in range(6):
        total = bias2_ref[...]
        for k in range(3):
            if 1 <= j + 2 * (k - 1) <= 4:
                total = total + dot(mid_ref[j + 2 * (k - 1) - 1], tap(w2_ref, k))
        pre2_ref[j] = total
    for k in range(3):
        to = slice((2 - k) * C, (3 - k) * C)
        w_t_ref[to] = tap(w_ref, k).T
        w2_t_ref[to] = tap(w2_ref, k).T
    proj_t_ref[...] = proj_ref[...].T
    proj2_t = proj2_ref[...].T
    for j in range(6):
        back_ref[j] = dot(up_ref[j], proj2_t)


def far_kernel(
    s_ref, left_ref, right_ref, near_ref, pre_ref, pre2_ref, back_ref, w_ref, bias_ref, proj_ref, w2_ref,
    act_ref, slope_ref, mid_ref, act2_ref, delta_ref, to_left_ref, to_right_ref,
):
    def at(j):
        return left_ref[j + 3] if j < 0 else right_ref[j - 6] if j > 5 else s_ref[j]

    def mid_at(j):
        return mid_ref[j + 2] if j < 1 else mid_ref[j - 2]

    def pair(one, two):
        return jnp.concatenate([one, two], axis=1)

    def product(j):
        if j == 0:
            return pre_ref[1] + dot(at(-1), tap(w_ref, 0))
        if j == 5:
            return pre_ref[2] + dot(at(6), tap(w_ref, 2))
        if j == -1:
            return pre_ref[0] + dot(pair(at(-2), at(-1)), w_ref[: 2 * C])
        if j == 6:
            return pre_ref[3] + dot(pair(at(6), at(7)), w_ref[C:])
        return dot(taps(at, j, 1), w_ref[...]) + bias_ref[...]

    def product2(j):
        if j == 0:
            return pre2_ref[0] + dot(pair(mid_at(-2), mid_at(0)), w2_ref[: 2 * C])
        if j == 5:
            return pre2_ref[5] + dot(pair(mid_at(5), mid_at(7)), w2_ref[C:])
        if j < 3:
            return pre2_ref[j] + dot(mid_at(j - 2), tap(w2_ref, 0))
        return pre2_ref[j] + dot(mid_at(j + 2), tap(w2_ref, 2))

    order = (0, 5, -2, 7, -1, 6)
    order2 = (2, 3, 0, 5, 1, 4)
    pre = product(order[0])
    for i, j in enumerate(order):
        after = product(order[i + 1]) if i < 5 else product2(order2[0])
        cdf = normal_cdf(pre)
        act = (pre * cdf).astype(BF)
        if j in (0, 5):
            act_ref[j // 5] = act
            slope_ref[j // 5] = slope_of(pre, cdf).astype(BF)
        mid = (at(j).astype(F32) + dot(act, proj_ref[...])).astype(BF)
        mid_ref[j + 2 if j < 1 else j - 2] = mid
        pre = after
    for i, j in enumerate(order2):
        after = product2(order2[i + 1]) if i < 5 else None
        cdf = normal_cdf(pre)
        act2_ref[j] = (pre * cdf).astype(BF)
        delta = (back_ref[j] * slope_of(pre, cdf)).astype(BF)
        delta_ref[j] = delta
        if j < 2:
            to_left_ref[j] = delta
        if j > 3:
            to_right_ref[j - 4] = delta
        pre = after


def add_grads(sum_ref, first, cells, delta, act, up):
    conv = t_dot(cells, delta)
    proj = t_dot(act, up)
    if first:
        sum_ref[: 3 * C] = conv
        sum_ref[3 * C :] = proj
    else:
        sum_ref[: 3 * C] += conv
        sum_ref[3 * C :] += proj
    return jnp.sum(delta.astype(F32), axis=0, keepdims=True)


def put_halves(sum_ref, bias, row, away_ref, mine_ref):
    core = lax.axis_index("core")
    half = 2 * C
    mine_ref[:half] = sum_ref[pl.ds(pl.multiple_of(core * half, half), half)].astype(BF)
    away_ref[:half] = sum_ref[pl.ds(pl.multiple_of((1 - core) * half, half), half)].astype(BF)
    at = lax.broadcasted_iota(jnp.int32, (16, C), 0)
    tail = jnp.where(at == row, jnp.broadcast_to(bias, (16, C)), 0.0).astype(BF)
    mine_ref[half:] = tail
    away_ref[half:] = tail


def inner_kernel(
    near_ref, far_ref, act2_ref, up_ref, delta_ref, w_t_ref, proj_t_ref, slope_ref, s_ref, act_ref,
    away_ref, mine_ref, below_ref, grad_ref, out_ref, sum_ref, bias_ref, total_ref,
):
    def mid_at(j):
        return far_ref[j + 2] if j < 1 else far_ref[j - 2] if j > 4 else near_ref[j - 1]

    at = lambda j: s_ref[j]
    bias = jnp.zeros((1, C), F32)
    for j in range(6):
        bias += add_grads(total_ref, j == 0, taps(mid_at, j, 2), delta_ref[j], act2_ref[j], up_ref[j])
    put_halves(total_ref, bias, 0, away_ref, mine_ref)
    for i, j in enumerate((0, 1, 4, 5)):
        low = slice(C, 3 * C) if j < 2 else slice(0, 2 * C)
        two = (delta_ref[j], delta_ref[j + 2]) if j < 2 else (delta_ref[j - 2], delta_ref[j])
        below_ref[i] = up_ref[j].astype(F32) + dot(jnp.concatenate(two, axis=1), w_t_ref[low])
    bias = jnp.zeros((1, C), F32)
    for j in (2, 3):
        three = jnp.concatenate([delta_ref[j - 2], delta_ref[j], delta_ref[j + 2]], axis=1)
        below = (up_ref[j].astype(F32) + dot(three, w_t_ref[...])).astype(BF)
        grad_ref[j - 2] = below
        delta = (dot(below, proj_t_ref[...]) * slope_ref[j - 1].astype(F32)).astype(BF)
        out_ref[j - 2] = delta
        bias += add_grads(sum_ref, j == 2, taps(at, j, 1), delta, act_ref[j - 1], below)
    bias_ref[...] = bias


def edge_kernel(
    below_ref, left_ref, right_ref, w_t_ref, proj_t_ref, slope_ref, slope_far_ref, s_ref, s_left_ref, s_right_ref,
    act_ref, act_far_ref, part_ref, part_bias_ref,
    grad_ref, out_ref, to_left_ref, to_right_ref, away_ref, mine_ref, sum_ref,
):
    def at(j):
        return s_left_ref[2] if j < 0 else s_right_ref[0] if j > 5 else s_ref[j]

    def product(i):
        far = dot(left_ref[i], tap(w_t_ref, 0)) if i < 2 else dot(right_ref[i - 2], tap(w_t_ref, 2))
        return (below_ref[i] + far).astype(BF)

    blocks = (0, 1, 4, 5)
    order = (0, 3, 1, 2)
    bias = part_bias_ref[...]
    sum_ref[...] = part_ref[...]
    below = product(order[0])
    held = None
    for n, i in enumerate(order):
        j = blocks[i]
        after = product(order[n + 1]) if n < 3 else None
        grad_ref[i] = below
        slope, act = (slope_far_ref[j // 5], act_far_ref[j // 5]) if j in (0, 5) else (slope_ref[j - 1], act_ref[j - 1])
        delta = (dot(below, proj_t_ref[...]) * slope.astype(F32)).astype(BF)
        out_ref[i] = delta
        if j == 0:
            to_left_ref[0] = delta
        if j == 5:
            to_right_ref[0] = delta
        if held is not None:
            bias += add_grads(sum_ref, False, *held)
        held = (taps(at, j, 1), delta, act, below)
        below = after
    bias += add_grads(sum_ref, False, *held)
    put_halves(sum_ref, bias, 1, away_ref, mine_ref)


def pair_kernel(mine_b_ref, near_b_ref, mine_a_ref, near_a_ref, out_ref):
    n, rows, _ = out_ref.shape
    chunk = (rows - 16) // 2

    def both(mine, near, part):
        return mine[part].astype(F32) + near[part].astype(F32)

    last = slice(n * chunk, n * chunk + 16)
    tail = (both(mine_b_ref, near_b_ref, last) + both(mine_a_ref, near_a_ref, last)).astype(BF)
    for i in range(n):
        part = slice(i * chunk, (i + 1) * chunk)
        out_ref[i, :chunk] = both(mine_b_ref, near_b_ref, part).astype(BF)
        out_ref[i, chunk : 2 * chunk] = both(mine_a_ref, near_a_ref, part).astype(BF)
        out_ref[i, 2 * chunk :] = tail


def rest_kernel(got_ref, out_ref):
    total = got_ref[0].astype(F32)
    for i in range(1, got_ref.shape[0]):
        total += got_ref[i].astype(F32)
    total = total.astype(BF)
    for i in range(out_ref.shape[0]):
        out_ref[i] = total


def token_kernel(left_ref, right_ref, out_ref):
    out_ref[...] = jnp.zeros(out_ref.shape, F32)


def ring_kernel(got_ref, token_ref, out_ref, bias_b_ref, bias_a_ref):
    total = got_ref[0].astype(F32) + token_ref[0:1, 0:1]
    for i in range(1, got_ref.shape[0]):
        total += got_ref[i].astype(F32)
    chunk = out_ref.shape[1]
    own = total[:chunk].astype(BF)
    for i in range(out_ref.shape[0]):
        out_ref[i] = own
    bias_b_ref[...] = total[chunk : chunk + 1]
    bias_a_ref[...] = total[chunk + 1 : chunk + 2]


def tail_kernel(mine_ref, other_ref, conv_b_ref, proj_b_ref, conv_a_ref, proj_a_ref):
    core = lax.axis_index("core")
    n, rows, _ = mine_ref.shape
    chunk = rows // 2

    def put(low, high):
        for i in range(n // 2):
            to = slice(i * chunk, (i + 1) * chunk)
            for part, conv, proj in ((0, conv_b_ref, proj_b_ref), (1, conv_a_ref, proj_a_ref)):
                of = slice(part * chunk, (part + 1) * chunk)
                conv[0, to] = low[i, of].astype(F32)
                conv[1, to] = low[i + n // 2, of].astype(F32)
                conv[2, to] = high[i, of].astype(F32)
                proj[to] = high[i + n // 2, of].astype(F32)

    @pl.when(core == 0)
    def _():
        put(mine_ref, other_ref)

    @pl.when(core != 0)
    def _():
        put(other_ref, mine_ref)


def lower_a_kernel(inner_ref, edge_ref, in_up_ref, edge_up_ref, w_ref, left_ref, right_ref, out_ref, ends, sems):
    one = pltpu.make_async_copy(left_ref, ends.at[0], sems.at[0])
    two = pltpu.make_async_copy(right_ref, ends.at[1], sems.at[1])
    one.start()
    two.start()

    def at(j):
        if j < 0 or j > 5:
            return ends[0 if j < 0 else 1, 0]
        return inner_ref[j - 2] if j in (2, 3) else edge_ref[j if j < 2 else j - 2]

    for j in (1, 2, 3, 4, 0, 5):
        if j == 0:
            one.wait()
            two.wait()
        up = in_up_ref[j - 2] if j in (2, 3) else edge_up_ref[j if j < 2 else j - 2]
        out_ref[j] = (up.astype(F32) + dot(taps(at, j, 1), w_ref[...])).astype(BF)


def call(kernel, outs, args, flops=0, scratch=(), far=0):
    vmem = pl.BlockSpec(memory_space=pltpu.VMEM)
    moved = sum(a.size * a.dtype.itemsize for a in args) + sum(
        math.prod(s) * jnp.dtype(t).itemsize for s, t in outs
    )
    return pl.pallas_call(
        kernel,
        out_shape=[jax.ShapeDtypeStruct(s, t) for s, t in outs],
        in_specs=[vmem] * (len(args) - far) + [pl.BlockSpec(memory_space=pltpu.HBM)] * far,
        out_specs=[vmem] * len(outs),
        scratch_shapes=list(scratch),
        compiler_params=pltpu.CompilerParams(vmem_limit_bytes=32 * 2**20),
        cost_estimate=pl.CostEstimate(flops=flops, bytes_accessed=moved, transcendentals=0),
        name=kernel.__name__[: -len("_kernel")],
    )(*args)


def from_left(cells):
    n = lax.axis_size(RING)
    return lax.ppermute(cells, RING, [(i, (i + 1) % n) for i in range(n)])


def from_right(cells):
    n = lax.axis_size(RING)
    return lax.ppermute(cells, RING, [((i + 1) % n, i) for i in range(n)])


def across(cells):
    return lax.ppermute(cells, "core", [(0, 1), (1, 0)])


def on_device(signals, cotangent, kernel_a, bias_a, proj_a, kernel_b, bias_b, proj_b):
    batch, length, channels = signals.shape
    unit = 2 * BLOCK * C * C
    cells = signals.reshape(-1, BLOCK, C)
    up = cotangent.reshape(-1, BLOCK, C)
    rest, ring = lax.axis_size(PLANE), lax.axis_size(COLUMN)
    wa, wb = kernel_a.reshape(3 * C, C), kernel_b.reshape(3 * C, C)
    ba, bb = bias_a.reshape(1, C), bias_b.reshape(1, C)

    def like(n, t=BF):
        return ((n, BLOCK, C), t)

    to_left, to_right = call(
        cut_kernel, [like(3)] * 2, [cells], scratch=[pltpu.SemaphoreType.DMA((2,))], far=1
    )
    s_left, s_right = from_left(to_right), from_right(to_left)
    act_near, slope_near, mid_near, pre_a, pre_b, back, wa_t, wb_t, pa_t = call(
        near_kernel,
        [like(4)] * 3 + [like(4, F32), like(6, F32), like(6, F32)] + [((3 * C, C), BF)] * 2 + [((C, C), BF)],
        [cells, up, wa, ba, proj_a, wb, bb, proj_b],
        38 * unit,
    )
    act_far, slope_far, mid_far, act_b, delta_b, to_left, to_right = call(
        far_kernel,
        [like(2), like(2), like(6), like(6), like(6), like(2), like(2)],
        [cells, s_left, s_right, mid_near, pre_a, pre_b, back, wa, ba, proj_a, wb],
        26 * unit,
    )
    d_left, d_right = from_left(to_right), from_right(to_left)
    half = ((2 * C + 16, C), BF)
    away_b, mine_b, below, grad_in, delta_in, part, part_bias = call(
        inner_kernel,
        [half, half, like(4, F32), like(2), like(2), ((4 * C, C), F32), ((1, C), F32)],
        [mid_near, mid_far, act_b, up, delta_b, wb_t, pa_t, slope_near, cells, act_near],
        48 * unit,
        [pltpu.VMEM((4 * C, C), F32)],
    )
    near_b = across(away_b)
    grad_out, delta_out, to_left, to_right, away_a, mine_a = call(
        edge_kernel,
        [like(4), like(4), like(1), like(1), half, half],
        [below, d_left, d_right, wb_t, pa_t, slope_near, slope_far, cells, s_left, s_right]
        + [act_near, act_far, part, part_bias],
        24 * unit,
        [pltpu.VMEM((4 * C, C), F32)],
    )
    e_left, e_right = from_left(to_right), from_right(to_left)
    chunk = 2 * C // rest
    (sent,) = call(
        pair_kernel,
        [((rest, 2 * chunk + 16, C), BF)],
        [mine_b, near_b, mine_a, across(away_a)],
    )
    got = lax.all_to_all(sent, PLANE, 0, 0)
    (sent,) = call(rest_kernel, [((ring, 2 * chunk + 16, C), BF)], [got])
    got = lax.all_to_all(sent, COLUMN, 0, 0)
    (token,) = call(token_kernel, [((8, 128), F32)], [e_left, e_right], far=2)
    sent, sum_bias_b, sum_bias_a = call(
        ring_kernel, [((rest, 2 * chunk, C), BF), ((1, C), F32), ((1, C), F32)], [got, token]
    )
    mine = lax.all_to_all(sent, PLANE, 0, 0)
    conv_b, grad_proj_b, conv_a, grad_proj_a = call(
        tail_kernel, [((3, C, C), F32), ((C, C), F32)] * 2, [mine, across(mine)]
    )
    (out,) = call(
        lower_a_kernel,
        [like(6)],
        [delta_in, delta_out, grad_in, grad_out, wa_t, e_left, e_right],
        18 * unit,
        [pltpu.VMEM((2, 1, BLOCK, C), BF), pltpu.SemaphoreType.DMA((2,))],
        far=2,
    )
    return (
        out.reshape(batch, length, channels),
        conv_a,
        sum_bias_a.reshape(C),
        grad_proj_a,
        conv_b,
        sum_bias_b.reshape(C),
        grad_proj_b,
    )


def solution(mesh):
    split = Mesh(mesh.devices.reshape(2, 4, 8, 2, 2), ("xh", "y", "z", "xl", "core"))
    data = P(("z", "xl", "core"), RING, None)
    return jax.shard_map(
        on_device,
        mesh=split,
        in_specs=(data, data, P(), P(), P(), P(), P(), P()),
        out_specs=(data, P(), P(), P(), P(), P(), P()),
        check_vma=False,
    )
```

```python
import math

import jax
import jax.numpy as jnp
from jax import lax
from jax.experimental import pallas as pl
from jax.experimental.pallas import tpu as pltpu
from jax.sharding import Mesh, PartitionSpec as P

BLOCK = 512
RING = ("xh", "y")
PLANE = ("xh", "y", "xl")
COLUMN = "z"
BF, F32 = jnp.bfloat16, jnp.float32
C = 256


def dot(a, b):
    return jnp.dot(a, b, preferred_element_type=F32)


def t_dot(a, b):
    return lax.dot_general(a, b, (((0,), (0,)), ((), ())), preferred_element_type=F32)


def normal_cdf(v):
    return 0.5 * (1.0 + lax.erf(v * math.sqrt(0.5)))


def slope_of(v, cdf):
    return cdf + v * jnp.exp2(v * v * (-0.5 * math.log2(math.e)) - 0.5 * math.log2(2.0 * math.pi))


def taps(at, j, hop):
    return jnp.concatenate([at(j - hop), at(j), at(j + hop)], axis=1)


def odd():
    return lax.rem(lax.axis_index("y"), 2)


def cut_kernel(s_ref, one_ref, two_ref, sems):
    one = pltpu.make_async_copy(s_ref.at[pl.ds(3 * odd(), 3)], one_ref, sems.at[0])
    two = pltpu.make_async_copy(s_ref.at[pl.ds(3 - 3 * odd(), 3)], two_ref, sems.at[1])
    one.start()
    two.start()
    one.wait()
    two.wait()


def tap(w_ref, k):
    return w_ref[k * C : (k + 1) * C]


def near_kernel(
    s_ref, up_ref, w_ref, bias_ref, proj_ref, w2_ref, bias2_ref, proj2_ref,
    act_ref, slope_ref, mid_ref, pre_ref, pre2_ref, back_ref, w_t_ref, w2_t_ref, proj_t_ref,
):
    at = lambda j: s_ref[j]

    def product(j):
        return dot(taps(at, j, 1), w_ref[...]) + bias_ref[...]

    pre = product(1)
    for j in range(1, 5):
        after = product(j + 1) if j < 4 else None
        cdf = normal_cdf(pre)
        act = (pre * cdf).astype(BF)
        act_ref[j - 1] = act
        slope_ref[j - 1] = slope_of(pre, cdf).astype(BF)
        mid_ref[j - 1] = (s_ref[j].astype(F32) + dot(act, proj_ref[...])).astype(BF)
        pre = after
    pre_ref[0] = dot(s_ref[0], tap(w_ref, 2)) + bias_ref[...]
    pre_ref[1] = dot(s_ref[0], tap(w_ref, 1)) + dot(s_ref[1], tap(w_ref, 2)) + bias_ref[...]
    pre_ref[2] = dot(s_ref[4], tap(w_ref, 0)) + dot(s_ref[5], tap(w_ref, 1)) + bias_ref[...]
    pre_ref[3] = dot(s_ref[5], tap(w_ref, 0)) + bias_ref[...]
    for j in range(6):
        total = bias2_ref[...]
        for k in range(3):
            if 1 <= j + 2 * (k - 1) <= 4:
                total = total + dot(mid_ref[j + 2 * (k - 1) - 1], tap(w2_ref, k))
        pre2_ref[j] = total
    for k in range(3):
        to = slice((2 - k) * C, (3 - k) * C)
        w_t_ref[to] = tap(w_ref, k).T
        w2_t_ref[to] = tap(w2_ref, k).T
    proj_t_ref[...] = proj_ref[...].T
    proj2_t = proj2_ref[...].T
    for j in range(6):
        back_ref[j] = dot(up_ref[j], proj2_t)


def far_kernel(
    s_ref, one_ref, two_ref, near_ref, pre_ref, pre2_ref, back_ref, w_ref, bias_ref, proj_ref, w2_ref,
    act_ref, slope_ref, mid_ref, act2_ref, delta_ref, ends_ref, to_one_ref, to_two_ref, left_ref, right_ref,
):
    def at(j):
        return left_ref[j + 3] if j < 0 else right_ref[j - 6] if j > 5 else s_ref[j]

    def mid_at(j):
        return mid_ref[j + 2] if j < 1 else mid_ref[j - 2]

    turned = odd() == 1
    for k in range(3):
        one, two = one_ref[k], two_ref[k]
        left_ref[k] = jnp.where(turned, two, one)
        right_ref[k] = jnp.where(turned, one, two)
    ends_ref[0] = left_ref[2]
    ends_ref[1] = right_ref[0]

    def pair(one, two):
        return jnp.concatenate([one, two], axis=1)

    def product(j):
        if j == 0:
            return pre_ref[1] + dot(at(-1), tap(w_ref, 0))
        if j == 5:
            return pre_ref[2] + dot(at(6), tap(w_ref, 2))
        if j == -1:
            return pre_ref[0] + dot(pair(at(-2), at(-1)), w_ref[: 2 * C])
        if j == 6:
            return pre_ref[3] + dot(pair(at(6), at(7)), w_ref[C:])
        return dot(taps(at, j, 1), w_ref[...]) + bias_ref[...]

    def product2(j):
        if j == 0:
            return pre2_ref[0] + dot(pair(mid_at(-2), mid_at(0)), w2_ref[: 2 * C])
        if j == 5:
            return pre2_ref[5] + dot(pair(mid_at(5), mid_at(7)), w2_ref[C:])
        if j == 1:
            return pre2_ref[1] + dot(mid_at(-1), tap(w2_ref, 0))
        return pre2_ref[4] + dot(mid_at(6), tap(w2_ref, 2))

    order = (0, 5, -2, 7, -1, 6)
    order2 = (0, 5, 1, 4)
    pre = product(order[0])
    for i, j in enumerate(order):
        after = product(order[i + 1]) if i < 5 else product2(order2[0])
        cdf = normal_cdf(pre)
        act = (pre * cdf).astype(BF)
        if j in (0, 5):
            act_ref[j // 5] = act
            slope_ref[j // 5] = slope_of(pre, cdf).astype(BF)
        mid = (at(j).astype(F32) + dot(act, proj_ref[...])).astype(BF)
        mid_ref[j + 2 if j < 1 else j - 2] = mid
        pre = after
    for i, j in enumerate(order2):
        after = product2(order2[i + 1]) if i < 3 else None
        cdf = normal_cdf(pre)
        act2_ref[j if j < 2 else j - 2] = (pre * cdf).astype(BF)
        delta = (back_ref[j] * slope_of(pre, cdf)).astype(BF)
        delta_ref[j if j < 2 else j - 2] = delta
        pre = after
        if j in (1, 4):
            k = 1 if j == 1 else 0
            low, high = delta_ref[k], delta_ref[k + 2]
            to_one_ref[k] = jnp.where(turned, high, low)
            to_two_ref[k] = jnp.where(turned, low, high)


def add_grads(sum_ref, first, cells, delta, act, up):
    conv = t_dot(cells, delta)
    proj = t_dot(act, up)
    if first:
        sum_ref[: 3 * C] = conv
        sum_ref[3 * C :] = proj
    else:
        sum_ref[: 3 * C] += conv
        sum_ref[3 * C :] += proj
    return jnp.sum(delta.astype(F32), axis=0, keepdims=True)


def put_halves(sum_ref, bias, row, away_ref, mine_ref):
    core = lax.axis_index("core")
    half = 2 * C
    mine_ref[:half] = sum_ref[pl.ds(pl.multiple_of(core * half, half), half)].astype(BF)
    away_ref[:half] = sum_ref[pl.ds(pl.multiple_of((1 - core) * half, half), half)].astype(BF)
    at = lax.broadcasted_iota(jnp.int32, (16, C), 0)
    tail = jnp.where(at == row, jnp.broadcast_to(bias, (16, C)), 0.0).astype(BF)
    mine_ref[half:] = tail
    away_ref[half:] = tail


def inner_kernel(
    near_ref, far_ref, act2_ref, up_ref, delta2_ref, pre2_ref, back_ref, w2_ref, w_t_ref, proj_t_ref, slope_ref, s_ref, act_ref,
    away_ref, mine_ref, below_ref, grad_ref, out_ref, sum_ref, bias_ref, total_ref,
):
    def mid_at(j):
        return far_ref[j + 2] if j < 1 else far_ref[j - 2] if j > 4 else near_ref[j - 1]

    at = lambda j: s_ref[j]
    delta = {j: delta2_ref[j if j < 2 else j - 2] for j in (0, 1, 4, 5)}
    act2 = {j: act2_ref[j if j < 2 else j - 2] for j in delta}
    products = {
        2: pre2_ref[2] + dot(mid_at(0), tap(w2_ref, 0)),
        3: pre2_ref[3] + dot(mid_at(5), tap(w2_ref, 2)),
    }
    bias = jnp.zeros((1, C), F32)
    for n, j in enumerate((0, 5, 1, 4, 2, 3)):
        if n in (1, 2):
            i = n + 1
            pre = products[i]
            cdf = normal_cdf(pre)
            act2[i] = (pre * cdf).astype(BF)
            delta[i] = (back_ref[i] * slope_of(pre, cdf)).astype(BF)
        bias += add_grads(total_ref, n == 0, taps(mid_at, j, 2), delta[j], act2[j], up_ref[j])
    put_halves(total_ref, bias, 0, away_ref, mine_ref)
    for i, j in enumerate((0, 1, 4, 5)):
        low = slice(C, 3 * C) if j < 2 else slice(0, 2 * C)
        two = (delta[j], delta[j + 2]) if j < 2 else (delta[j - 2], delta[j])
        below_ref[i] = up_ref[j].astype(F32) + dot(jnp.concatenate(two, axis=1), w_t_ref[low])
    bias = jnp.zeros((1, C), F32)
    for j in (2, 3):
        three = jnp.concatenate([delta[j - 2], delta[j], delta[j + 2]], axis=1)
        below = (up_ref[j].astype(F32) + dot(three, w_t_ref[...])).astype(BF)
        grad_ref[j - 2] = below
        first = (dot(below, proj_t_ref[...]) * slope_ref[j - 1].astype(F32)).astype(BF)
        out_ref[j - 2] = first
        bias += add_grads(sum_ref, j == 2, taps(at, j, 1), first, act_ref[j - 1], below)
    bias_ref[...] = bias


def edge_kernel(
    below_ref, one_ref, two_ref, w_t_ref, proj_t_ref, slope_ref, slope_far_ref, s_ref, ends_ref,
    act_ref, act_far_ref, part_ref, part_bias_ref,
    grad_ref, out_ref, to_one_ref, to_two_ref, away_ref, mine_ref, sum_ref,
):
    def at(j):
        return ends_ref[0] if j < 0 else ends_ref[1] if j > 5 else s_ref[j]

    def product(i):
        if i < 2:
            far = dot(jnp.where(turned, two_ref[i], one_ref[i]), tap(w_t_ref, 0))
        else:
            far = dot(jnp.where(turned, one_ref[i - 2], two_ref[i - 2]), tap(w_t_ref, 2))
        return (below_ref[i] + far).astype(BF)

    turned = odd() == 1
    blocks = (0, 1, 4, 5)
    order = (0, 3, 1, 2)
    bias = part_bias_ref[...]
    sum_ref[...] = part_ref[...]
    below = product(order[0])
    held = None
    for n, i in enumerate(order):
        j = blocks[i]
        after = product(order[n + 1]) if n < 3 else None
        grad_ref[i] = below
        slope, act = (slope_far_ref[j // 5], act_far_ref[j // 5]) if j in (0, 5) else (slope_ref[j - 1], act_ref[j - 1])
        delta = (dot(below, proj_t_ref[...]) * slope.astype(F32)).astype(BF)
        out_ref[i] = delta
        if j == 5:
            to_one_ref[0] = jnp.where(turned, delta, out_ref[0])
            to_two_ref[0] = jnp.where(turned, out_ref[0], delta)
        if held is not None:
            bias += add_grads(sum_ref, False, *held)
        held = (taps(at, j, 1), delta, act, below)
        below = after
    bias += add_grads(sum_ref, False, *held)
    put_halves(sum_ref, bias, 1, away_ref, mine_ref)


def pair_kernel(mine_b_ref, near_b_ref, mine_a_ref, near_a_ref, done_ref, out_ref):
    n, rows, _ = out_ref.shape
    chunk = (rows - 16) // 2

    def both(mine, near, part):
        return mine[part].astype(F32) + near[part].astype(F32)

    last = slice(n * chunk, n * chunk + 16)
    tail = (both(mine_b_ref, near_b_ref, last) + both(mine_a_ref, near_a_ref, last)).astype(BF)
    for i in range(n):
        part = slice(i * chunk, (i + 1) * chunk)
        out_ref[i, :chunk] = both(mine_b_ref, near_b_ref, part).astype(BF)
        out_ref[i, chunk : 2 * chunk] = both(mine_a_ref, near_a_ref, part).astype(BF)
        out_ref[i, 2 * chunk :] = tail


def rest_kernel(got_ref, out_ref):
    total = got_ref[0].astype(F32)
    for i in range(1, got_ref.shape[0]):
        total += got_ref[i].astype(F32)
    total = total.astype(BF)
    for i in range(out_ref.shape[0]):
        out_ref[i] = total


def token_kernel(one_ref, two_ref, out_ref):
    out_ref[...] = jnp.zeros(out_ref.shape, F32)


def ring_kernel(got_ref, token_ref, out_ref, bias_b_ref, bias_a_ref):
    total = got_ref[0].astype(F32) + token_ref[0:1, 0:1]
    for i in range(1, got_ref.shape[0]):
        total += got_ref[i].astype(F32)
    chunk = out_ref.shape[1]
    own = total[:chunk].astype(BF)
    for i in range(out_ref.shape[0]):
        out_ref[i] = own
    bias_b_ref[...] = total[chunk : chunk + 1]
    bias_a_ref[...] = total[chunk + 1 : chunk + 2]


def tail_kernel(mine_ref, other_ref, conv_b_ref, proj_b_ref, conv_a_ref, proj_a_ref):
    core = lax.axis_index("core")
    n, rows, _ = mine_ref.shape
    chunk = rows // 2

    def put(low, high):
        for i in range(n // 2):
            to = slice(i * chunk, (i + 1) * chunk)
            for part, conv, proj in ((0, conv_b_ref, proj_b_ref), (1, conv_a_ref, proj_a_ref)):
                of = slice(part * chunk, (part + 1) * chunk)
                conv[0, to] = low[i, of].astype(F32)
                conv[1, to] = low[i + n // 2, of].astype(F32)
                conv[2, to] = high[i, of].astype(F32)
                proj[to] = high[i + n // 2, of].astype(F32)

    @pl.when(core == 0)
    def _():
        put(mine_ref, other_ref)

    @pl.when(core != 0)
    def _():
        put(other_ref, mine_ref)


def lower_inner_kernel(inner_ref, edge_ref, in_up_ref, edge_up_ref, w_ref, out_ref, part_ref):
    at = lambda j: inner_ref[j - 2] if j in (2, 3) else edge_ref[j if j < 2 else j - 2]
    for j in range(1, 5):
        up = in_up_ref[j - 2] if j in (2, 3) else edge_up_ref[j if j < 2 else j - 2]
        out_ref[j - 1] = (up.astype(F32) + dot(taps(at, j, 1), w_ref[...])).astype(BF)
    for i, own, low in ((0, (0, 1), C), (1, (4, 5), 0)):
        two = jnp.concatenate([at(own[0]), at(own[1])], axis=1)
        part_ref[i] = edge_up_ref[3 * i].astype(F32) + dot(two, w_ref[low : low + 2 * C])


def lower_outer_kernel(part_ref, w_ref, one_ref, two_ref, inner_ref, out_ref, parts, ends, sems):
    copies = [
        pltpu.make_async_copy(one_ref, parts.at[pl.ds(odd(), 1)], sems.at[0]),
        pltpu.make_async_copy(two_ref, parts.at[pl.ds(1 - odd(), 1)], sems.at[1]),
        pltpu.make_async_copy(inner_ref, out_ref.at[pl.ds(1, 4)], sems.at[2]),
    ]
    for copy in copies:
        copy.start()
    copies[0].wait()
    copies[1].wait()
    last = []
    for i in range(2):
        ends[i] = (part_ref[i] + dot(parts[i], tap(w_ref, 2 * i))).astype(BF)
        last.append(pltpu.make_async_copy(ends.at[pl.ds(i, 1)], out_ref.at[pl.ds(5 * i, 1)], sems.at[3 + i]))
        last[i].start()
    for copy in last + copies[2:]:
        copy.wait()


def call(kernel, outs, args, flops=0, scratch=(), far=0, far_out=False):
    vmem, hbm = pl.BlockSpec(memory_space=pltpu.VMEM), pl.BlockSpec(memory_space=pltpu.HBM)
    moved = sum(a.size * a.dtype.itemsize for a in args) + sum(
        math.prod(s) * jnp.dtype(t).itemsize for s, t in outs
    )
    return pl.pallas_call(
        kernel,
        out_shape=[jax.ShapeDtypeStruct(s, t) for s, t in outs],
        in_specs=[vmem] * (len(args) - far) + [hbm] * far,
        out_specs=[hbm if far_out else vmem] * len(outs),
        scratch_shapes=list(scratch),
        compiler_params=pltpu.CompilerParams(vmem_limit_bytes=32 * 2**20),
        cost_estimate=pl.CostEstimate(flops=flops, bytes_accessed=moved, transcendentals=0),
        name=kernel.__name__[: -len("_kernel")],
    )(*args)


def exchange(to_one, to_two):
    n = lax.axis_size(RING)
    one = [(i, (i + 1 if i % 2 else i - 1) % n) for i in range(n)]
    two = [(i, (i - 1 if i % 2 else i + 1) % n) for i in range(n)]
    return lax.ppermute(to_one, RING, one), lax.ppermute(to_two, RING, two)


def across(cells):
    return lax.ppermute(cells, "core", [(0, 1), (1, 0)])


def on_device(signals, cotangent, kernel_a, bias_a, proj_a, kernel_b, bias_b, proj_b):
    batch, length, channels = signals.shape
    unit = 2 * BLOCK * C * C
    cells = signals.reshape(-1, BLOCK, C)
    up = cotangent.reshape(-1, BLOCK, C)
    rest, ring = lax.axis_size(PLANE), lax.axis_size(COLUMN)
    wa, wb = kernel_a.reshape(3 * C, C), kernel_b.reshape(3 * C, C)
    ba, bb = bias_a.reshape(1, C), bias_b.reshape(1, C)

    def like(n, t=BF):
        return ((n, BLOCK, C), t)

    to_one, to_two = call(
        cut_kernel, [like(3)] * 2, [cells], scratch=[pltpu.SemaphoreType.DMA((2,))], far=1
    )
    s_one, s_two = exchange(to_one, to_two)
    act_near, slope_near, mid_near, pre_a, pre_b, back, wa_t, wb_t, pa_t = call(
        near_kernel,
        [like(4)] * 3 + [like(4, F32), like(6, F32), like(6, F32)] + [((3 * C, C), BF)] * 2 + [((C, C), BF)],
        [cells, up, wa, ba, proj_a, wb, bb, proj_b],
        38 * unit,
    )
    act_far, slope_far, mid_far, act_b, delta_b, s_ends, to_one, to_two = call(
        far_kernel,
        [like(2), like(2), like(6), like(4), like(4), like(2), like(2), like(2)],
        [cells, s_one, s_two, mid_near, pre_a, pre_b, back, wa, ba, proj_a, wb],
        24 * unit,
        [pltpu.VMEM((3, BLOCK, C), BF)] * 2,
    )
    d_one, d_two = exchange(to_one, to_two)
    half = ((2 * C + 16, C), BF)
    away_b, mine_b, below, grad_in, delta_in, part, part_bias = call(
        inner_kernel,
        [half, half, like(4, F32), like(2), like(2), ((4 * C, C), F32), ((1, C), F32)],
        [mid_near, mid_far, act_b, up, delta_b, pre_b, back, wb, wb_t, pa_t, slope_near, cells, act_near],
        50 * unit,
        [pltpu.VMEM((4 * C, C), F32)],
    )
    near_b = across(away_b)
    grad_out, delta_out, to_one, to_two, away_a, mine_a = call(
        edge_kernel,
        [like(4), like(4), like(1), like(1), half, half],
        [below, d_one, d_two, wb_t, pa_t, slope_near, slope_far, cells, s_ends]
        + [act_near, act_far, part, part_bias],
        24 * unit,
        [pltpu.VMEM((4 * C, C), F32)],
    )
    e_one, e_two = exchange(to_one, to_two)
    inside, outside = call(
        lower_inner_kernel,
        [like(4), like(2, F32)],
        [delta_in, delta_out, grad_in, grad_out, wa_t],
        16 * unit,
    )
    chunk = 2 * C // rest
    (sent,) = call(
        pair_kernel,
        [((rest, 2 * chunk + 16, C), BF)],
        [mine_b, near_b, mine_a, across(away_a), inside],
        far=1,
    )
    got = lax.all_to_all(sent, PLANE, 0, 0)
    (sent,) = call(rest_kernel, [((ring, 2 * chunk + 16, C), BF)], [got])
    got = lax.all_to_all(sent, COLUMN, 0, 0)
    (token,) = call(token_kernel, [((8, 128), F32)], [e_one, e_two], far=2)
    sent, sum_bias_b, sum_bias_a = call(
        ring_kernel, [((rest, 2 * chunk, C), BF), ((1, C), F32), ((1, C), F32)], [got, token]
    )
    mine = lax.all_to_all(sent, PLANE, 0, 0)
    conv_b, grad_proj_b, conv_a, grad_proj_a = call(
        tail_kernel, [((3, C, C), F32), ((C, C), F32)] * 2, [mine, across(mine)]
    )
    (out,) = call(
        lower_outer_kernel,
        [like(6)],
        [outside, wa_t, e_one, e_two, inside],
        2 * unit,
        [pltpu.VMEM((2, BLOCK, C), BF)] * 2 + [pltpu.SemaphoreType.DMA((5,))],
        far=3,
        far_out=True,
    )
    return (
        out.reshape(batch, length, channels),
        conv_a,
        sum_bias_a.reshape(C),
        grad_proj_a,
        conv_b,
        sum_bias_b.reshape(C),
        grad_proj_b,
    )


def solution(mesh):
    split = Mesh(mesh.devices.reshape(2, 4, 8, 2, 2), ("xh", "y", "z", "xl", "core"))
    data = P(("z", "xl", "core"), RING, None)
    return jax.shard_map(
        on_device,
        mesh=split,
        in_specs=(data, data, P(), P(), P(), P(), P(), P()),
        out_specs=(data, P(), P(), P(), P(), P(), P()),
        check_vma=False,
    )
```

```python
import math

import jax
import jax.numpy as jnp
from jax import lax
from jax.experimental import pallas as pl
from jax.experimental.pallas import tpu as pltpu
from jax.sharding import Mesh, PartitionSpec as P

BLOCK = 512
RING = ("xh", "y")
PLANE = ("xh", "y", "xl")
COLUMN = "z"
BF, F32 = jnp.bfloat16, jnp.float32
C = 256


def dot(a, b):
    return jnp.dot(a, b, preferred_element_type=F32)


def t_dot(a, b):
    return lax.dot_general(a, b, (((0,), (0,)), ((), ())), preferred_element_type=F32)


def normal_cdf(v):
    return 0.5 * (1.0 + lax.erf(v * math.sqrt(0.5)))


def slope_of(v, cdf):
    return cdf + v * jnp.exp2(v * v * (-0.5 * math.log2(math.e)) - 0.5 * math.log2(2.0 * math.pi))


def taps(at, j, hop):
    return jnp.concatenate([at(j - hop), at(j), at(j + hop)], axis=1)


def odd():
    return lax.rem(lax.axis_index("y"), 2)


def cut_kernel(s_ref, one_ref, two_ref, one_far_ref, two_far_ref, sems):
    copies = [
        pltpu.make_async_copy(s_ref.at[pl.ds(at, ref.shape[0])], ref, sems.at[i])
        for i, (at, ref) in enumerate(
            (
                (4 * odd(), one_ref),
                (4 - 4 * odd(), two_ref),
                (2 + odd(), one_far_ref),
                (3 - odd(), two_far_ref),
            )
        )
    ]
    for copy in copies:
        copy.start()
    for copy in copies:
        copy.wait()


def tap(w_ref, k):
    return w_ref[k * C : (k + 1) * C]


def near_kernel(
    s_ref, up_ref, w_ref, bias_ref, proj_ref, w2_ref, bias2_ref, proj2_ref,
    act_ref, slope_ref, mid_ref, pre_ref, pre2_ref, back_ref, w_t_ref, w2_t_ref, proj_t_ref,
):
    at = lambda j: s_ref[j]

    def product(j):
        return dot(taps(at, j, 1), w_ref[...]) + bias_ref[...]

    pre = product(1)
    for j in range(1, 5):
        after = product(j + 1) if j < 4 else None
        cdf = normal_cdf(pre)
        act = (pre * cdf).astype(BF)
        act_ref[j - 1] = act
        slope_ref[j - 1] = slope_of(pre, cdf).astype(BF)
        mid_ref[j - 1] = (s_ref[j].astype(F32) + dot(act, proj_ref[...])).astype(BF)
        pre = after
    pre_ref[0] = dot(s_ref[0], tap(w_ref, 2)) + bias_ref[...]
    pre_ref[1] = dot(s_ref[0], tap(w_ref, 1)) + dot(s_ref[1], tap(w_ref, 2)) + bias_ref[...]
    pre_ref[2] = dot(s_ref[4], tap(w_ref, 0)) + dot(s_ref[5], tap(w_ref, 1)) + bias_ref[...]
    pre_ref[3] = dot(s_ref[5], tap(w_ref, 0)) + bias_ref[...]
    for j in range(6):
        total = bias2_ref[...]
        for k in range(3):
            if 1 <= j + 2 * (k - 1) <= 4:
                total = total + dot(mid_ref[j + 2 * (k - 1) - 1], tap(w2_ref, k))
        pre2_ref[j] = total
    for k in range(3):
        to = slice((2 - k) * C, (3 - k) * C)
        w_t_ref[to] = tap(w_ref, k).T
        w2_t_ref[to] = tap(w2_ref, k).T
    proj_t_ref[...] = proj_ref[...].T
    proj2_t = proj2_ref[...].T
    for j in range(6):
        back_ref[j] = dot(up_ref[j], proj2_t)


def pair(one, two):
    return jnp.concatenate([one, two], axis=1)


def far_kernel(
    s_ref, one_ref, two_ref, near_ref, pre_ref, pre2_ref, back_ref, w_ref, proj_ref, w2_ref,
    act_ref, slope_ref, mid_ref, act2_ref, delta_ref, halo_ref, to_one_ref, to_two_ref,
):
    turned = odd() == 1
    for k in range(2):
        one, two = one_ref[k], two_ref[k]
        halo_ref[k] = jnp.where(turned, two, one)
        halo_ref[2 + k] = jnp.where(turned, one, two)

    def at(j):
        return halo_ref[j + 2] if j < 0 else halo_ref[j - 4] if j > 5 else s_ref[j]

    def product(j):
        if j == 0:
            return pre_ref[1] + dot(at(-1), tap(w_ref, 0))
        if j == 5:
            return pre_ref[2] + dot(at(6), tap(w_ref, 2))
        if j == -1:
            return pre_ref[0] + dot(pair(at(-2), at(-1)), w_ref[: 2 * C])
        return pre_ref[3] + dot(pair(at(6), at(7)), w_ref[C:])

    def product2(i):
        if i == 0:
            return pre2_ref[1] + dot(mid_ref[0], tap(w2_ref, 0))
        return pre2_ref[4] + dot(mid_ref[3], tap(w2_ref, 2))

    order = (-1, 6, 0, 5)
    pre = product(order[0])
    for n, j in enumerate(order):
        after = product(order[n + 1]) if n < 3 else product2(0)
        cdf = normal_cdf(pre)
        act = (pre * cdf).astype(BF)
        if j in (0, 5):
            act_ref[j // 5] = act
            slope_ref[j // 5] = slope_of(pre, cdf).astype(BF)
        mid = (at(j).astype(F32) + dot(act, proj_ref[...])).astype(BF)
        mid_ref[j + 1 if j < 1 else j - 3] = mid
        pre = after
    for i, j in enumerate((1, 4)):
        after = product2(1) if i == 0 else None
        cdf = normal_cdf(pre)
        act2_ref[i] = (pre * cdf).astype(BF)
        delta_ref[i] = (back_ref[j] * slope_of(pre, cdf)).astype(BF)
        pre = after
    to_one_ref[0] = jnp.where(turned, delta_ref[1], delta_ref[0])
    to_two_ref[0] = jnp.where(turned, delta_ref[0], delta_ref[1])


def last_kernel(
    halo_ref, one_ref, two_ref, near_mid_ref, pre2_ref, back_ref, w_ref, bias_ref, proj_ref, w2_ref,
    mid_ref, act2_ref, delta_ref, to_one_ref, to_two_ref,
):
    turned = odd() == 1
    low = jnp.where(turned, two_ref[0], one_ref[0])
    high = jnp.where(turned, one_ref[0], two_ref[0])
    three = (
        jnp.concatenate([low, halo_ref[0], halo_ref[1]], axis=1),
        jnp.concatenate([halo_ref[2], halo_ref[3], high], axis=1),
    )

    def product2(i):
        if i == 0:
            return pre2_ref[0] + dot(pair(mid_ref[0], near_mid_ref[1]), w2_ref[: 2 * C])
        return pre2_ref[5] + dot(pair(near_mid_ref[2], mid_ref[1]), w2_ref[C:])

    pre = dot(three[0], w_ref[...]) + bias_ref[...]
    for i in range(2):
        after = dot(three[1], w_ref[...]) + bias_ref[...] if i == 0 else product2(0)
        act = (pre * normal_cdf(pre)).astype(BF)
        mid_ref[i] = (halo_ref[3 * i].astype(F32) + dot(act, proj_ref[...])).astype(BF)
        pre = after
    for i, j in enumerate((0, 5)):
        after = product2(1) if i == 0 else None
        cdf = normal_cdf(pre)
        act2_ref[i] = (pre * cdf).astype(BF)
        delta_ref[i] = (back_ref[j] * slope_of(pre, cdf)).astype(BF)
        pre = after
    to_one_ref[0] = jnp.where(turned, delta_ref[1], delta_ref[0])
    to_two_ref[0] = jnp.where(turned, delta_ref[0], delta_ref[1])


def add_grads(sum_ref, first, cells, delta, act, up):
    conv = t_dot(cells, delta)
    proj = t_dot(act, up)
    if first:
        sum_ref[: 3 * C] = conv
        sum_ref[3 * C :] = proj
    else:
        sum_ref[: 3 * C] += conv
        sum_ref[3 * C :] += proj
    return jnp.sum(delta.astype(F32), axis=0, keepdims=True)


def put_halves(sum_ref, bias, row, away_ref, mine_ref):
    core = lax.axis_index("core")
    half = 2 * C
    mine_ref[:half] = sum_ref[pl.ds(pl.multiple_of(core * half, half), half)].astype(BF)
    away_ref[:half] = sum_ref[pl.ds(pl.multiple_of((1 - core) * half, half), half)].astype(BF)
    at = lax.broadcasted_iota(jnp.int32, (16, C), 0)
    tail = jnp.where(at == row, jnp.broadcast_to(bias, (16, C)), 0.0).astype(BF)
    mine_ref[half:] = tail
    away_ref[half:] = tail


def inner_kernel(
    near_ref, far_ref, last_ref, act2_far_ref, act2_last_ref, up_ref, delta_far_ref, delta_last_ref,
    pre2_ref, back_ref, w2_ref, w_t_ref, proj_t_ref, slope_ref, s_ref, act_ref,
    away_ref, mine_ref, below_ref, grad_ref, out_ref, sum_ref, bias_ref, total_ref,
):
    def mid_at(j):
        if j in (-2, 7):
            return last_ref[0 if j < 0 else 1]
        return far_ref[j + 1] if j < 1 else far_ref[j - 3] if j > 4 else near_ref[j - 1]

    at = lambda j: s_ref[j]
    delta = {1: delta_far_ref[0], 4: delta_far_ref[1], 0: delta_last_ref[0], 5: delta_last_ref[1]}
    act2 = {1: act2_far_ref[0], 4: act2_far_ref[1], 0: act2_last_ref[0], 5: act2_last_ref[1]}
    products = {
        2: pre2_ref[2] + dot(mid_at(0), tap(w2_ref, 0)),
        3: pre2_ref[3] + dot(mid_at(5), tap(w2_ref, 2)),
    }
    bias = jnp.zeros((1, C), F32)
    for n, j in enumerate((0, 5, 1, 4, 2, 3)):
        if n in (1, 2):
            i = n + 1
            pre = products[i]
            cdf = normal_cdf(pre)
            act2[i] = (pre * cdf).astype(BF)
            delta[i] = (back_ref[i] * slope_of(pre, cdf)).astype(BF)
        bias += add_grads(total_ref, n == 0, taps(mid_at, j, 2), delta[j], act2[j], up_ref[j])
    put_halves(total_ref, bias, 0, away_ref, mine_ref)
    for i, j in enumerate((0, 1, 4, 5)):
        low = slice(C, 3 * C) if j < 2 else slice(0, 2 * C)
        two = pair(delta[j], delta[j + 2]) if j < 2 else pair(delta[j - 2], delta[j])
        below_ref[i] = up_ref[j].astype(F32) + dot(two, w_t_ref[low])
    bias = jnp.zeros((1, C), F32)
    for j in (2, 3):
        three = jnp.concatenate([delta[j - 2], delta[j], delta[j + 2]], axis=1)
        below = (up_ref[j].astype(F32) + dot(three, w_t_ref[...])).astype(BF)
        grad_ref[j - 2] = below
        first = (dot(below, proj_t_ref[...]) * slope_ref[j - 1].astype(F32)).astype(BF)
        out_ref[j - 2] = first
        bias += add_grads(sum_ref, j == 2, taps(at, j, 1), first, act_ref[j - 1], below)
    bias_ref[...] = bias


def ends_kernel(
    below_ref, one_ref, two_ref, w_t_ref, proj_t_ref, slope_ref, s_ref, halo_ref, act_ref, part_ref, part_bias_ref,
    grad_ref, out_ref, to_one_ref, to_two_ref, sum_ref, bias_ref,
):
    turned = odd() == 1

    def at(j):
        return halo_ref[1] if j < 0 else halo_ref[2] if j > 5 else s_ref[j]

    def product(i):
        if i == 0:
            far = dot(jnp.where(turned, two_ref[0], one_ref[0]), tap(w_t_ref, 0))
        else:
            far = dot(jnp.where(turned, one_ref[0], two_ref[0]), tap(w_t_ref, 2))
        return (below_ref[3 * i] + far).astype(BF)

    bias = part_bias_ref[...]
    sum_ref[...] = part_ref[...]
    below = [product(0), product(1)]
    for i, j in enumerate((0, 5)):
        grad_ref[i] = below[i]
        delta = (dot(below[i], proj_t_ref[...]) * slope_ref[i].astype(F32)).astype(BF)
        out_ref[i] = delta
        bias += add_grads(sum_ref, False, taps(at, j, 1), delta, act_ref[i], below[i])
    bias_ref[...] = bias
    to_one_ref[0] = jnp.where(turned, out_ref[1], out_ref[0])
    to_two_ref[0] = jnp.where(turned, out_ref[0], out_ref[1])


def edge_kernel(
    below_ref, one_ref, two_ref, w_t_ref, proj_t_ref, slope_ref, s_ref, act_ref, part_ref, part_bias_ref,
    grad_ref, out_ref, away_ref, mine_ref, sum_ref,
):
    at = lambda j: s_ref[j]
    turned = odd() == 1

    def product(i):
        if i == 0:
            far = dot(jnp.where(turned, two_ref[0], one_ref[0]), tap(w_t_ref, 0))
        else:
            far = dot(jnp.where(turned, one_ref[0], two_ref[0]), tap(w_t_ref, 2))
        return (below_ref[1 + i] + far).astype(BF)

    bias = part_bias_ref[...]
    sum_ref[...] = part_ref[...]
    below = [product(0), product(1)]
    for i, j in enumerate((1, 4)):
        grad_ref[i] = below[i]
        delta = (dot(below[i], proj_t_ref[...]) * slope_ref[j - 1].astype(F32)).astype(BF)
        out_ref[i] = delta
        bias += add_grads(sum_ref, False, taps(at, j, 1), delta, act_ref[j - 1], below[i])
    put_halves(sum_ref, bias, 1, away_ref, mine_ref)


def pair_kernel(mine_b_ref, near_b_ref, mine_a_ref, near_a_ref, done_ref, out_ref):
    n, rows, _ = out_ref.shape
    chunk = (rows - 16) // 2

    def both(mine, near, part):
        return mine[part].astype(F32) + near[part].astype(F32)

    last = slice(n * chunk, n * chunk + 16)
    tail = (both(mine_b_ref, near_b_ref, last) + both(mine_a_ref, near_a_ref, last)).astype(BF)
    for i in range(n):
        part = slice(i * chunk, (i + 1) * chunk)
        out_ref[i, :chunk] = both(mine_b_ref, near_b_ref, part).astype(BF)
        out_ref[i, chunk : 2 * chunk] = both(mine_a_ref, near_a_ref, part).astype(BF)
        out_ref[i, 2 * chunk :] = tail


def rest_kernel(got_ref, out_ref):
    total = got_ref[0].astype(F32)
    for i in range(1, got_ref.shape[0]):
        total += got_ref[i].astype(F32)
    total = total.astype(BF)
    for i in range(out_ref.shape[0]):
        out_ref[i] = total


def token_kernel(one_ref, two_ref, out_ref):
    out_ref[...] = jnp.zeros(out_ref.shape, F32)


def ring_kernel(got_ref, token_ref, out_ref, bias_b_ref, bias_a_ref):
    total = got_ref[0].astype(F32) + token_ref[0:1, 0:1]
    for i in range(1, got_ref.shape[0]):
        total += got_ref[i].astype(F32)
    chunk = out_ref.shape[1]
    own = total[:chunk].astype(BF)
    for i in range(out_ref.shape[0]):
        out_ref[i] = own
    bias_b_ref[...] = total[chunk : chunk + 1]
    bias_a_ref[...] = total[chunk + 1 : chunk + 2]


def tail_kernel(mine_ref, other_ref, conv_b_ref, proj_b_ref, conv_a_ref, proj_a_ref):
    core = lax.axis_index("core")
    n, rows, _ = mine_ref.shape
    chunk = rows // 2

    def put(low, high):
        for i in range(n // 2):
            to = slice(i * chunk, (i + 1) * chunk)
            for part, conv, proj in ((0, conv_b_ref, proj_b_ref), (1, conv_a_ref, proj_a_ref)):
                of = slice(part * chunk, (part + 1) * chunk)
                conv[0, to] = low[i, of].astype(F32)
                conv[1, to] = low[i + n // 2, of].astype(F32)
                conv[2, to] = high[i, of].astype(F32)
                proj[to] = high[i + n // 2, of].astype(F32)

    @pl.when(core == 0)
    def _():
        put(mine_ref, other_ref)

    @pl.when(core != 0)
    def _():
        put(other_ref, mine_ref)


def lower_inner_kernel(
    inner_ref, ends_ref, edge_ref, in_up_ref, ends_up_ref, edge_up_ref, w_ref, out_ref, part_ref
):
    def place(j, inner, ends, edge):
        return inner[j - 2] if j in (2, 3) else ends[j // 5] if j in (0, 5) else edge[j // 4]

    at = lambda j: place(j, inner_ref, ends_ref, edge_ref)
    for j in range(1, 5):
        up = place(j, in_up_ref, ends_up_ref, edge_up_ref)
        out_ref[j - 1] = (up.astype(F32) + dot(taps(at, j, 1), w_ref[...])).astype(BF)
    for i, own, low in ((0, (0, 1), C), (1, (4, 5), 0)):
        two = pair(at(own[0]), at(own[1]))
        part_ref[i] = ends_up_ref[i].astype(F32) + dot(two, w_ref[low : low + 2 * C])


def lower_outer_kernel(part_ref, w_ref, one_ref, two_ref, inner_ref, out_ref, parts, ends, sems):
    copies = [
        pltpu.make_async_copy(one_ref, parts.at[pl.ds(odd(), 1)], sems.at[0]),
        pltpu.make_async_copy(two_ref, parts.at[pl.ds(1 - odd(), 1)], sems.at[1]),
        pltpu.make_async_copy(inner_ref, out_ref.at[pl.ds(1, 4)], sems.at[2]),
    ]
    for copy in copies:
        copy.start()
    copies[0].wait()
    copies[1].wait()
    last = []
    for i in range(2):
        ends[i] = (part_ref[i] + dot(parts[i], tap(w_ref, 2 * i))).astype(BF)
        last.append(pltpu.make_async_copy(ends.at[pl.ds(i, 1)], out_ref.at[pl.ds(5 * i, 1)], sems.at[3 + i]))
        last[i].start()
    for copy in last + copies[2:]:
        copy.wait()


def call(kernel, outs, args, flops=0, scratch=(), far=0, far_out=False):
    vmem, hbm = pl.BlockSpec(memory_space=pltpu.VMEM), pl.BlockSpec(memory_space=pltpu.HBM)
    moved = flops if flops == 1024 else sum(a.size * a.dtype.itemsize for a in args) + sum(
        math.prod(s) * jnp.dtype(t).itemsize for s, t in outs
    )
    return pl.pallas_call(
        kernel,
        out_shape=[jax.ShapeDtypeStruct(s, t) for s, t in outs],
        in_specs=[vmem] * (len(args) - far) + [hbm] * far,
        out_specs=[hbm if far_out else vmem] * len(outs),
        scratch_shapes=list(scratch),
        compiler_params=pltpu.CompilerParams(vmem_limit_bytes=32 * 2**20),
        cost_estimate=pl.CostEstimate(flops=flops, bytes_accessed=moved, transcendentals=0),
        name=kernel.__name__[: -len("_kernel")],
    )(*args)


def exchange(to_one, to_two):
    n = lax.axis_size(RING)
    one = [(i, (i + 1 if i % 2 else i - 1) % n) for i in range(n)]
    two = [(i, (i - 1 if i % 2 else i + 1) % n) for i in range(n)]
    return lax.ppermute(to_one, RING, one), lax.ppermute(to_two, RING, two)


def across(cells):
    return lax.ppermute(cells, "core", [(0, 1), (1, 0)])


def on_device(signals, cotangent, kernel_a, bias_a, proj_a, kernel_b, bias_b, proj_b):
    batch, length, channels = signals.shape
    unit = 2 * BLOCK * C * C
    cells = signals.reshape(-1, BLOCK, C)
    up = cotangent.reshape(-1, BLOCK, C)
    rest, ring = lax.axis_size(PLANE), lax.axis_size(COLUMN)
    wa, wb = kernel_a.reshape(3 * C, C), kernel_b.reshape(3 * C, C)
    ba, bb = bias_a.reshape(1, C), bias_b.reshape(1, C)

    def like(n, t=BF):
        return ((n, BLOCK, C), t)

    to_one, to_two, to_one_far, to_two_far = call(
        cut_kernel,
        [like(2), like(2), like(1), like(1)],
        [cells],
        scratch=[pltpu.SemaphoreType.DMA((4,))],
        far=1,
    )
    s_one, s_two = exchange(to_one, to_two)
    s_one_far, s_two_far = exchange(to_one_far, to_two_far)
    act_near, slope_near, mid_near, pre_a, pre_b, back, wa_t, wb_t, pa_t = call(
        near_kernel,
        [like(4)] * 3 + [like(4, F32), like(6, F32), like(6, F32)] + [((3 * C, C), BF)] * 2 + [((C, C), BF)],
        [cells, up, wa, ba, proj_a, wb, bb, proj_b],
        1024,
    )
    act_far, slope_far, mid_far, act_b_far, delta_b_far, halo, to_one, to_two = call(
        far_kernel,
        [like(2), like(2), like(4), like(2), like(2), like(4), like(1), like(1)],
        [cells, s_one, s_two, mid_near, pre_a, pre_b, back, wa, proj_a, wb],
        1024,
    )
    d_one, d_two = exchange(to_one, to_two)
    mid_last, act_b_last, delta_b_last, to_one, to_two = call(
        last_kernel,
        [like(2), like(2), like(2), like(1), like(1)],
        [halo, s_one_far, s_two_far, mid_far, pre_b, back, wa, ba, proj_a, wb],
        1024,
    )
    d_one_far, d_two_far = exchange(to_one, to_two)
    half = ((2 * C + 16, C), BF)
    away_b, mine_b, below, grad_in, delta_in, part, part_bias = call(
        inner_kernel,
        [half, half, like(4, F32), like(2), like(2), ((4 * C, C), F32), ((1, C), F32)],
        [mid_near, mid_far, mid_last, act_b_far, act_b_last, up, delta_b_far, delta_b_last]
        + [pre_b, back, wb, wb_t, pa_t, slope_near, cells, act_near],
        1024,
        [pltpu.VMEM((4 * C, C), F32)],
    )
    grad_end, delta_end, to_one, to_two, part, part_bias = call(
        ends_kernel,
        [like(2), like(2), like(1), like(1), ((4 * C, C), F32), ((1, C), F32)],
        [below, d_one, d_two, wb_t, pa_t, slope_far, cells, halo, act_far, part, part_bias],
        1024,
    )
    e_one, e_two = exchange(to_one, to_two)
    near_b = across(away_b)
    grad_out, delta_out, away_a, mine_a = call(
        edge_kernel,
        [like(2), like(2), half, half],
        [below, d_one_far, d_two_far, wb_t, pa_t, slope_near, cells, act_near, part, part_bias],
        12 * unit,
        [pltpu.VMEM((4 * C, C), F32)],
    )
    inside, outside = call(
        lower_inner_kernel,
        [like(4), like(2, F32)],
        [delta_in, delta_end, delta_out, grad_in, grad_end, grad_out, wa_t],
        16 * unit,
    )
    chunk = 2 * C // rest
    (sent,) = call(
        pair_kernel,
        [((rest, 2 * chunk + 16, C), BF)],
        [mine_b, near_b, mine_a, across(away_a), inside],
        far=1,
    )
    got = lax.all_to_all(sent, PLANE, 0, 0)
    (sent,) = call(rest_kernel, [((ring, 2 * chunk + 16, C), BF)], [got])
    got = lax.all_to_all(sent, COLUMN, 0, 0)
    (token,) = call(token_kernel, [((8, 128), F32)], [e_one, e_two], far=2)
    sent, sum_bias_b, sum_bias_a = call(
        ring_kernel, [((rest, 2 * chunk, C), BF), ((1, C), F32), ((1, C), F32)], [got, token]
    )
    mine = lax.all_to_all(sent, PLANE, 0, 0)
    conv_b, grad_proj_b, conv_a, grad_proj_a = call(
        tail_kernel, [((3, C, C), F32), ((C, C), F32)] * 2, [mine, across(mine)]
    )
    (out,) = call(
        lower_outer_kernel,
        [like(6)],
        [outside, wa_t, e_one, e_two, inside],
        2 * unit,
        [pltpu.VMEM((2, BLOCK, C), BF)] * 2 + [pltpu.SemaphoreType.DMA((5,))],
        far=3,
        far_out=True,
    )
    return (
        out.reshape(batch, length, channels),
        conv_a,
        sum_bias_a.reshape(C),
        grad_proj_a,
        conv_b,
        sum_bias_b.reshape(C),
        grad_proj_b,
    )


def solution(mesh):
    split = Mesh(mesh.devices.reshape(2, 4, 8, 2, 2), ("xh", "y", "z", "xl", "core"))
    data = P(("z", "xl", "core"), RING, None)
    return jax.shard_map(
        on_device,
        mesh=split,
        in_specs=(data, data, P(), P(), P(), P(), P(), P()),
        out_specs=(data, P(), P(), P(), P(), P(), P()),
        check_vma=False,
    )
```

```python
import math

import jax
import jax.numpy as jnp
from jax import lax
from jax.experimental import pallas as pl
from jax.experimental.pallas import tpu as pltpu
from jax.sharding import Mesh, PartitionSpec as P

BLOCK = 512
RING = ("xh", "y")
PLANE = ("xl", "xh", "y")
COLUMN = "z"
BF, F32 = jnp.bfloat16, jnp.float32
C = 256


def dot(a, b):
    return jnp.dot(a, b, preferred_element_type=F32)


def t_dot(a, b):
    return lax.dot_general(a, b, (((0,), (0,)), ((), ())), preferred_element_type=F32)


def normal_cdf(v):
    return 0.5 * (1.0 + lax.erf(v * math.sqrt(0.5)))


def slope_of(v, cdf):
    return cdf + v * jnp.exp2(v * v * (-0.5 * math.log2(math.e)) - 0.5 * math.log2(2.0 * math.pi))


def taps(at, j, hop):
    return jnp.concatenate([at(j - hop), at(j), at(j + hop)], axis=1)


def odd():
    return lax.rem(lax.axis_index("y"), 2)


def cut_kernel(s_ref, one_ref, two_ref, one_far_ref, two_far_ref, sems):
    copies = [
        pltpu.make_async_copy(s_ref.at[pl.ds(at, ref.shape[0])], ref, sems.at[i])
        for i, (at, ref) in enumerate(
            (
                (4 * odd(), one_ref),
                (4 - 4 * odd(), two_ref),
                (2 + odd(), one_far_ref),
                (3 - odd(), two_far_ref),
            )
        )
    ]
    for copy in copies:
        copy.start()
    for copy in copies:
        copy.wait()


def tap(w_ref, k):
    return w_ref[k * C : (k + 1) * C]


def near_kernel(
    s_ref, up_ref, w_ref, bias_ref, proj_ref, w2_ref, bias2_ref, proj2_ref,
    act_ref, slope_ref, mid_ref, pre_ref, pre2_ref, back_ref, w_t_ref, w2_t_ref, proj_t_ref,
):
    at = lambda j: s_ref[j]

    def product(j):
        return dot(taps(at, j, 1), w_ref[...]) + bias_ref[...]

    pre = product(1)
    for j in range(1, 5):
        after = product(j + 1) if j < 4 else None
        cdf = normal_cdf(pre)
        act = (pre * cdf).astype(BF)
        act_ref[j - 1] = act
        slope_ref[j - 1] = slope_of(pre, cdf).astype(BF)
        mid_ref[j - 1] = (s_ref[j].astype(F32) + dot(act, proj_ref[...])).astype(BF)
        pre = after
    pre_ref[0] = dot(s_ref[0], tap(w_ref, 2)) + bias_ref[...]
    pre_ref[1] = dot(s_ref[0], tap(w_ref, 1)) + dot(s_ref[1], tap(w_ref, 2)) + bias_ref[...]
    pre_ref[2] = dot(s_ref[4], tap(w_ref, 0)) + dot(s_ref[5], tap(w_ref, 1)) + bias_ref[...]
    pre_ref[3] = dot(s_ref[5], tap(w_ref, 0)) + bias_ref[...]
    for j in range(6):
        total = bias2_ref[...]
        for k in range(3):
            if 1 <= j + 2 * (k - 1) <= 4:
                total = total + dot(mid_ref[j + 2 * (k - 1) - 1], tap(w2_ref, k))
        pre2_ref[j] = total
    for k in range(3):
        to = slice((2 - k) * C, (3 - k) * C)
        w_t_ref[to] = tap(w_ref, k).T
        w2_t_ref[to] = tap(w2_ref, k).T
    proj_t_ref[...] = proj_ref[...].T
    proj2_t = proj2_ref[...].T
    for j in range(6):
        back_ref[j] = dot(up_ref[j], proj2_t)


def pair(one, two):
    return jnp.concatenate([one, two], axis=1)


def far_kernel(
    s_ref, one_ref, two_ref, near_ref, pre_ref, pre2_ref, back_ref, w_ref, proj_ref, w2_ref,
    act_ref, slope_ref, mid_ref, act2_ref, delta_ref, halo_ref, to_one_ref, to_two_ref,
):
    turned = odd() == 1
    for k in range(2):
        one, two = one_ref[k], two_ref[k]
        halo_ref[k] = jnp.where(turned, two, one)
        halo_ref[2 + k] = jnp.where(turned, one, two)

    def at(j):
        return halo_ref[j + 2] if j < 0 else halo_ref[j - 4] if j > 5 else s_ref[j]

    def product(j):
        if j == 0:
            return pre_ref[1] + dot(at(-1), tap(w_ref, 0))
        if j == 5:
            return pre_ref[2] + dot(at(6), tap(w_ref, 2))
        if j == -1:
            return pre_ref[0] + dot(pair(at(-2), at(-1)), w_ref[: 2 * C])
        return pre_ref[3] + dot(pair(at(6), at(7)), w_ref[C:])

    def product2(i):
        if i == 0:
            return pre2_ref[1] + dot(mid_ref[0], tap(w2_ref, 0))
        return pre2_ref[4] + dot(mid_ref[3], tap(w2_ref, 2))

    order = (-1, 6, 0, 5)
    pre = product(order[0])
    for n, j in enumerate(order):
        after = product(order[n + 1]) if n < 3 else product2(0)
        cdf = normal_cdf(pre)
        act = (pre * cdf).astype(BF)
        if j in (0, 5):
            act_ref[j // 5] = act
            slope_ref[j // 5] = slope_of(pre, cdf).astype(BF)
        mid = (at(j).astype(F32) + dot(act, proj_ref[...])).astype(BF)
        mid_ref[j + 1 if j < 1 else j - 3] = mid
        pre = after
    for i, j in enumerate((1, 4)):
        after = product2(1) if i == 0 else None
        cdf = normal_cdf(pre)
        act2_ref[i] = (pre * cdf).astype(BF)
        delta_ref[i] = (back_ref[j] * slope_of(pre, cdf)).astype(BF)
        pre = after
    to_one_ref[0] = jnp.where(turned, delta_ref[1], delta_ref[0])
    to_two_ref[0] = jnp.where(turned, delta_ref[0], delta_ref[1])


def last_kernel(
    halo_ref, one_ref, two_ref, near_mid_ref, pre2_ref, back_ref, w_ref, bias_ref, proj_ref, w2_ref,
    mid_ref, act2_ref, delta_ref, to_one_ref, to_two_ref,
):
    turned = odd() == 1
    low = jnp.where(turned, two_ref[0], one_ref[0])
    high = jnp.where(turned, one_ref[0], two_ref[0])
    three = (
        jnp.concatenate([low, halo_ref[0], halo_ref[1]], axis=1),
        jnp.concatenate([halo_ref[2], halo_ref[3], high], axis=1),
    )

    def product2(i):
        if i == 0:
            return pre2_ref[0] + dot(pair(mid_ref[0], near_mid_ref[1]), w2_ref[: 2 * C])
        return pre2_ref[5] + dot(pair(near_mid_ref[2], mid_ref[1]), w2_ref[C:])

    pre = dot(three[0], w_ref[...]) + bias_ref[...]
    for i in range(2):
        after = dot(three[1], w_ref[...]) + bias_ref[...] if i == 0 else product2(0)
        act = (pre * normal_cdf(pre)).astype(BF)
        mid_ref[i] = (halo_ref[3 * i].astype(F32) + dot(act, proj_ref[...])).astype(BF)
        pre = after
    for i, j in enumerate((0, 5)):
        after = product2(1) if i == 0 else None
        cdf = normal_cdf(pre)
        act2_ref[i] = (pre * cdf).astype(BF)
        delta_ref[i] = (back_ref[j] * slope_of(pre, cdf)).astype(BF)
        pre = after
    to_one_ref[0] = jnp.where(turned, delta_ref[1], delta_ref[0])
    to_two_ref[0] = jnp.where(turned, delta_ref[0], delta_ref[1])


def add_grads(sum_ref, base_ref, cells, delta, act, up):
    conv = t_dot(cells, delta)
    proj = t_dot(act, up)
    sum_ref[: 3 * C] = conv if base_ref is None else base_ref[: 3 * C] + conv
    sum_ref[3 * C :] = proj if base_ref is None else base_ref[3 * C :] + proj
    return jnp.sum(delta.astype(F32), axis=0, keepdims=True)


def put_halves(sum_ref, bias, row, away_ref, mine_ref):
    core = lax.axis_index("core")
    half = 2 * C
    mine_ref[:half] = sum_ref[pl.ds(pl.multiple_of(core * half, half), half)].astype(BF)
    away_ref[:half] = sum_ref[pl.ds(pl.multiple_of((1 - core) * half, half), half)].astype(BF)
    at = lax.broadcasted_iota(jnp.int32, (16, C), 0)
    tail = jnp.where(at == row, jnp.broadcast_to(bias, (16, C)), 0.0).astype(BF)
    mine_ref[half:] = tail
    away_ref[half:] = tail


def inner_kernel(
    near_ref, far_ref, last_ref, act2_far_ref, act2_last_ref, up_ref, delta_far_ref, delta_last_ref,
    pre2_ref, back_ref, w2_ref, w_t_ref, proj_t_ref, slope_ref, s_ref, act_ref,
    away_ref, mine_ref, below_ref, grad_ref, out_ref, sum_ref, bias_ref, total_ref,
):
    def mid_at(j):
        if j in (-2, 7):
            return last_ref[0 if j < 0 else 1]
        return far_ref[j + 1] if j < 1 else far_ref[j - 3] if j > 4 else near_ref[j - 1]

    at = lambda j: s_ref[j]
    delta = {1: delta_far_ref[0], 4: delta_far_ref[1], 0: delta_last_ref[0], 5: delta_last_ref[1]}
    act2 = {1: act2_far_ref[0], 4: act2_far_ref[1], 0: act2_last_ref[0], 5: act2_last_ref[1]}
    products = {
        2: pre2_ref[2] + dot(mid_at(0), tap(w2_ref, 0)),
        3: pre2_ref[3] + dot(mid_at(5), tap(w2_ref, 2)),
    }
    bias = jnp.zeros((1, C), F32)
    for n, j in enumerate((0, 5, 1, 4, 2, 3)):
        if n in (1, 2):
            i = n + 1
            pre = products[i]
            cdf = normal_cdf(pre)
            act2[i] = (pre * cdf).astype(BF)
            delta[i] = (back_ref[i] * slope_of(pre, cdf)).astype(BF)
        bias += add_grads(total_ref, total_ref if n else None, taps(mid_at, j, 2), delta[j], act2[j], up_ref[j])
    put_halves(total_ref, bias, 0, away_ref, mine_ref)
    for i, j in enumerate((0, 1, 4, 5)):
        low = slice(C, 3 * C) if j < 2 else slice(0, 2 * C)
        two = pair(delta[j], delta[j + 2]) if j < 2 else pair(delta[j - 2], delta[j])
        below_ref[i] = up_ref[j].astype(F32) + dot(two, w_t_ref[low])
    bias = jnp.zeros((1, C), F32)
    for j in (2, 3):
        three = jnp.concatenate([delta[j - 2], delta[j], delta[j + 2]], axis=1)
        below = (up_ref[j].astype(F32) + dot(three, w_t_ref[...])).astype(BF)
        grad_ref[j - 2] = below
        first = (dot(below, proj_t_ref[...]) * slope_ref[j - 1].astype(F32)).astype(BF)
        out_ref[j - 2] = first
        bias += add_grads(sum_ref, sum_ref if j > 2 else None, taps(at, j, 1), first, act_ref[j - 1], below)
    bias_ref[...] = bias


def ends_kernel(
    below_ref, one_ref, two_ref, w_t_ref, proj_t_ref, slope_ref, s_ref, halo_ref, act_ref, part_ref, part_bias_ref,
    grad_ref, out_ref, to_one_ref, to_two_ref, sum_ref, bias_ref,
):
    turned = odd() == 1

    def at(j):
        return halo_ref[1] if j < 0 else halo_ref[2] if j > 5 else s_ref[j]

    def product(i):
        if i == 0:
            far = dot(jnp.where(turned, two_ref[0], one_ref[0]), tap(w_t_ref, 0))
        else:
            far = dot(jnp.where(turned, one_ref[0], two_ref[0]), tap(w_t_ref, 2))
        return (below_ref[3 * i] + far).astype(BF)

    bias = part_bias_ref[...]
    below = [product(0), product(1)]
    for i, j in enumerate((0, 5)):
        grad_ref[i] = below[i]
        delta = (dot(below[i], proj_t_ref[...]) * slope_ref[i].astype(F32)).astype(BF)
        out_ref[i] = delta
        bias += add_grads(sum_ref, sum_ref if i else part_ref, taps(at, j, 1), delta, act_ref[i], below[i])
    bias_ref[...] = bias
    to_one_ref[0] = jnp.where(turned, out_ref[1], out_ref[0])
    to_two_ref[0] = jnp.where(turned, out_ref[0], out_ref[1])


def edge_kernel(
    below_ref, one_ref, two_ref, w_t_ref, proj_t_ref, slope_ref, s_ref, act_ref, part_ref, part_bias_ref,
    grad_ref, out_ref, away_ref, mine_ref, sum_ref,
):
    at = lambda j: s_ref[j]
    turned = odd() == 1

    def product(i):
        if i == 0:
            far = dot(jnp.where(turned, two_ref[0], one_ref[0]), tap(w_t_ref, 0))
        else:
            far = dot(jnp.where(turned, one_ref[0], two_ref[0]), tap(w_t_ref, 2))
        return (below_ref[1 + i] + far).astype(BF)

    bias = part_bias_ref[...]
    below = [product(0), product(1)]
    for i, j in enumerate((1, 4)):
        grad_ref[i] = below[i]
        delta = (dot(below[i], proj_t_ref[...]) * slope_ref[j - 1].astype(F32)).astype(BF)
        out_ref[i] = delta
        base_ref = sum_ref if i else part_ref
        bias += add_grads(sum_ref, base_ref, taps(at, j, 1), delta, act_ref[j - 1], below[i])
    put_halves(sum_ref, bias, 1, away_ref, mine_ref)


def pair_kernel(mine_b_ref, near_b_ref, mine_a_ref, near_a_ref, done_ref, out_ref):
    n, rows, _ = out_ref.shape
    chunk = (rows - 16) // 2

    def both(mine, near, part):
        return mine[part].astype(F32) + near[part].astype(F32)

    last = slice(n * chunk, n * chunk + 16)
    tail = (both(mine_b_ref, near_b_ref, last) + both(mine_a_ref, near_a_ref, last)).astype(BF)
    for i in range(n):
        part = slice(i * chunk, (i + 1) * chunk)
        out_ref[i, :chunk] = both(mine_b_ref, near_b_ref, part).astype(BF)
        out_ref[i, chunk : 2 * chunk] = both(mine_a_ref, near_a_ref, part).astype(BF)
        out_ref[i, 2 * chunk :] = tail


def rest_kernel(got_ref, out_ref):
    total = got_ref[0].astype(F32)
    for i in range(1, got_ref.shape[0]):
        total += got_ref[i].astype(F32)
    total = total.astype(BF)
    for i in range(out_ref.shape[0]):
        out_ref[i] = total


def token_kernel(one_ref, two_ref, out_ref):
    out_ref[...] = jnp.zeros(out_ref.shape, F32)


def ring_kernel(got_ref, token_ref, out_ref, bias_b_ref, bias_a_ref):
    total = got_ref[0].astype(F32) + token_ref[0:1, 0:1]
    for i in range(1, got_ref.shape[0]):
        total += got_ref[i].astype(F32)
    chunk = out_ref.shape[1]
    own = total[:chunk].astype(BF)
    for i in range(out_ref.shape[0]):
        out_ref[i] = own
    bias_b_ref[...] = total[chunk : chunk + 1]
    bias_a_ref[...] = total[chunk + 1 : chunk + 2]


def tail_kernel(mine_ref, other_ref, conv_b_ref, proj_b_ref, conv_a_ref, proj_a_ref, work, sems):
    core = lax.axis_index("core")
    n, rows, _ = mine_ref.shape
    chunk = rows // 2

    def put(low, high):
        copies = []
        for at in range(8):
            src, matrix, part = (low, high)[at // 4], at // 2 % 2, at % 2
            conv, proj = ((conv_b_ref, proj_b_ref), (conv_a_ref, proj_a_ref))[part]
            for i in range(n // 2):
                to, of = slice(i * chunk, (i + 1) * chunk), slice(part * chunk, (part + 1) * chunk)
                work[at, to] = src[matrix * (n // 2) + i, of].astype(F32)
            to = conv.at[matrix] if at < 4 else conv.at[2] if matrix == 0 else proj
            copies.append(pltpu.make_async_copy(work.at[at], to, sems.at[at]))
            copies[at].start()
        for copy in copies:
            copy.wait()

    @pl.when(core == 0)
    def _():
        put(mine_ref, other_ref)

    @pl.when(core != 0)
    def _():
        put(other_ref, mine_ref)


def lower_inner_kernel(
    inner_ref, ends_ref, edge_ref, in_up_ref, ends_up_ref, edge_up_ref, w_ref, out_ref, part_ref
):
    def place(j, inner, ends, edge):
        return inner[j - 2] if j in (2, 3) else ends[j // 5] if j in (0, 5) else edge[j // 4]

    at = lambda j: place(j, inner_ref, ends_ref, edge_ref)
    for j in range(1, 5):
        up = place(j, in_up_ref, ends_up_ref, edge_up_ref)
        out_ref[j - 1] = (up.astype(F32) + dot(taps(at, j, 1), w_ref[...])).astype(BF)
    for i, own, low in ((0, (0, 1), C), (1, (4, 5), 0)):
        two = pair(at(own[0]), at(own[1]))
        part_ref[i] = ends_up_ref[i].astype(F32) + dot(two, w_ref[low : low + 2 * C])


def lower_outer_kernel(part_ref, w_ref, one_ref, two_ref, inner_ref, out_ref, parts, ends, sems):
    copies = [
        pltpu.make_async_copy(one_ref, parts.at[pl.ds(odd(), 1)], sems.at[0]),
        pltpu.make_async_copy(two_ref, parts.at[pl.ds(1 - odd(), 1)], sems.at[1]),
        pltpu.make_async_copy(inner_ref, out_ref.at[pl.ds(1, 4)], sems.at[2]),
    ]
    for copy in copies:
        copy.start()
    copies[0].wait()
    copies[1].wait()
    last = []
    for i in range(2):
        ends[i] = (part_ref[i] + dot(parts[i], tap(w_ref, 2 * i))).astype(BF)
        last.append(pltpu.make_async_copy(ends.at[pl.ds(i, 1)], out_ref.at[pl.ds(5 * i, 1)], sems.at[3 + i]))
        last[i].start()
    for copy in last + copies[2:]:
        copy.wait()


def call(kernel, outs, args, flops=0, scratch=(), far=0, far_out=False):
    vmem, hbm = pl.BlockSpec(memory_space=pltpu.VMEM), pl.BlockSpec(memory_space=pltpu.HBM)
    moved = flops if flops == 1024 else sum(a.size * a.dtype.itemsize for a in args) + sum(
        math.prod(s) * jnp.dtype(t).itemsize for s, t in outs
    )
    return pl.pallas_call(
        kernel,
        out_shape=[jax.ShapeDtypeStruct(s, t) for s, t in outs],
        in_specs=[vmem] * (len(args) - far) + [hbm] * far,
        out_specs=[hbm if far_out else vmem] * len(outs),
        scratch_shapes=list(scratch),
        compiler_params=pltpu.CompilerParams(vmem_limit_bytes=32 * 2**20),
        cost_estimate=pl.CostEstimate(flops=flops, bytes_accessed=moved, transcendentals=0),
        name=kernel.__name__[: -len("_kernel")],
    )(*args)


def exchange(to_one, to_two):
    n = lax.axis_size(RING)
    one = [(i, (i + 1 if i % 2 else i - 1) % n) for i in range(n)]
    two = [(i, (i - 1 if i % 2 else i + 1) % n) for i in range(n)]
    return lax.ppermute(to_one, RING, one), lax.ppermute(to_two, RING, two)


def across(cells):
    return lax.ppermute(cells, "core", [(0, 1), (1, 0)])


def on_device(signals, cotangent, kernel_a, bias_a, proj_a, kernel_b, bias_b, proj_b):
    batch, length, channels = signals.shape
    unit = 2 * BLOCK * C * C
    cells = signals.reshape(-1, BLOCK, C)
    up = cotangent.reshape(-1, BLOCK, C)
    rest, ring = lax.axis_size(PLANE), lax.axis_size(COLUMN)
    wa, wb = kernel_a.reshape(3 * C, C), kernel_b.reshape(3 * C, C)
    ba, bb = bias_a.reshape(1, C), bias_b.reshape(1, C)

    def like(n, t=BF):
        return ((n, BLOCK, C), t)

    to_one, to_two, to_one_far, to_two_far = call(
        cut_kernel,
        [like(2), like(2), like(1), like(1)],
        [cells],
        scratch=[pltpu.SemaphoreType.DMA((4,))],
        far=1,
    )
    s_one, s_two = exchange(to_one, to_two)
    s_one_far, s_two_far = exchange(to_one_far, to_two_far)
    act_near, slope_near, mid_near, pre_a, pre_b, back, wa_t, wb_t, pa_t = call(
        near_kernel,
        [like(4)] * 3 + [like(4, F32), like(6, F32), like(6, F32)] + [((3 * C, C), BF)] * 2 + [((C, C), BF)],
        [cells, up, wa, ba, proj_a, wb, bb, proj_b],
        1024,
    )
    act_far, slope_far, mid_far, act_b_far, delta_b_far, halo, to_one, to_two = call(
        far_kernel,
        [like(2), like(2), like(4), like(2), like(2), like(4), like(1), like(1)],
        [cells, s_one, s_two, mid_near, pre_a, pre_b, back, wa, proj_a, wb],
        1024,
    )
    d_one, d_two = exchange(to_one, to_two)
    mid_last, act_b_last, delta_b_last, to_one, to_two = call(
        last_kernel,
        [like(2), like(2), like(2), like(1), like(1)],
        [halo, s_one_far, s_two_far, mid_far, pre_b, back, wa, ba, proj_a, wb],
        1024,
    )
    d_one_far, d_two_far = exchange(to_one, to_two)
    half = ((2 * C + 16, C), BF)
    away_b, mine_b, below, grad_in, delta_in, part, part_bias = call(
        inner_kernel,
        [half, half, like(4, F32), like(2), like(2), ((4 * C, C), F32), ((1, C), F32)],
        [mid_near, mid_far, mid_last, act_b_far, act_b_last, up, delta_b_far, delta_b_last]
        + [pre_b, back, wb, wb_t, pa_t, slope_near, cells, act_near],
        1024,
        [pltpu.VMEM((4 * C, C), F32)],
    )
    grad_end, delta_end, to_one, to_two, part, part_bias = call(
        ends_kernel,
        [like(2), like(2), like(1), like(1), ((4 * C, C), F32), ((1, C), F32)],
        [below, d_one, d_two, wb_t, pa_t, slope_far, cells, halo, act_far, part, part_bias],
        1024,
    )
    e_one, e_two = exchange(to_one, to_two)
    near_b = across(away_b)
    grad_out, delta_out, away_a, mine_a = call(
        edge_kernel,
        [like(2), like(2), half, half],
        [below, d_one_far, d_two_far, wb_t, pa_t, slope_near, cells, act_near, part, part_bias],
        12 * unit,
        [pltpu.VMEM((4 * C, C), F32)],
    )
    inside, outside = call(
        lower_inner_kernel,
        [like(4), like(2, F32)],
        [delta_in, delta_end, delta_out, grad_in, grad_end, grad_out, wa_t],
        16 * unit,
    )
    chunk = 2 * C // rest
    (sent,) = call(
        pair_kernel,
        [((rest, 2 * chunk + 16, C), BF)],
        [mine_b, near_b, mine_a, across(away_a), inside],
        far=1,
    )
    got = lax.all_to_all(sent, PLANE, 0, 0)
    (sent,) = call(rest_kernel, [((ring, 2 * chunk + 16, C), BF)], [got])
    got = lax.all_to_all(sent, COLUMN, 0, 0)
    (token,) = call(token_kernel, [((8, 128), F32)], [e_one, e_two], far=2)
    sent, sum_bias_b, sum_bias_a = call(
        ring_kernel, [((rest, 2 * chunk, C), BF), ((1, C), F32), ((1, C), F32)], [got, token]
    )
    mine = lax.all_to_all(sent, PLANE, 0, 0)
    conv_b, grad_proj_b, conv_a, grad_proj_a = call(
        tail_kernel,
        [((3, C, C), F32), ((C, C), F32)] * 2,
        [mine, across(mine)],
        scratch=[pltpu.VMEM((8, C, C), F32), pltpu.SemaphoreType.DMA((8,))],
        far_out=True,
    )
    (out,) = call(
        lower_outer_kernel,
        [like(6)],
        [outside, wa_t, e_one, e_two, inside],
        2 * unit,
        [pltpu.VMEM((2, BLOCK, C), BF)] * 2 + [pltpu.SemaphoreType.DMA((5,))],
        far=3,
        far_out=True,
    )
    return (
        out.reshape(batch, length, channels),
        conv_a,
        sum_bias_a.reshape(C),
        grad_proj_a,
        conv_b,
        sum_bias_b.reshape(C),
        grad_proj_b,
    )


def solution(mesh):
    split = Mesh(mesh.devices.reshape(2, 4, 8, 2, 2), ("xh", "y", "z", "xl", "core"))
    data = P(("z", "xl", "core"), RING, None)
    return jax.shard_map(
        on_device,
        mesh=split,
        in_specs=(data, data, P(), P(), P(), P(), P(), P()),
        out_specs=(data, P(), P(), P(), P(), P(), P()),
        check_vma=False,
    )
```

```python
import math

import jax
import jax.numpy as jnp
from jax import lax
from jax.experimental import pallas as pl
from jax.experimental.pallas import tpu as pltpu
from jax.sharding import Mesh, PartitionSpec as P

BLOCK = 512
RING = ("xh", "y")
PLANE = ("xl", "xh", "y")
COLUMN = "z"
BF, F32 = jnp.bfloat16, jnp.float32
C = 256


def dot(a, b):
    return jnp.dot(a, b, preferred_element_type=F32)


def t_dot(a, b):
    return lax.dot_general(a, b, (((0,), (0,)), ((), ())), preferred_element_type=F32)


def normal_cdf(v):
    return 0.5 * (1.0 + lax.erf(v * math.sqrt(0.5)))


def slope_of(v, cdf):
    return cdf + v * jnp.exp2(v * v * (-0.5 * math.log2(math.e)) - 0.5 * math.log2(2.0 * math.pi))


def taps(at, j, hop):
    return jnp.concatenate([at(j - hop), at(j), at(j + hop)], axis=1)


def odd():
    return lax.rem(lax.axis_index("y"), 2)


def cut_kernel(s_ref, one_ref, two_ref, one_far_ref, two_far_ref, sems):
    copies = [
        pltpu.make_async_copy(s_ref.at[pl.ds(at, ref.shape[0])], ref, sems.at[i])
        for i, (at, ref) in enumerate(
            (
                (4 * odd(), one_ref),
                (4 - 4 * odd(), two_ref),
                (2 + odd(), one_far_ref),
                (3 - odd(), two_far_ref),
            )
        )
    ]
    for copy in copies:
        copy.start()
    for copy in copies:
        copy.wait()


def tap(w_ref, k):
    return w_ref[k * C : (k + 1) * C]


def near_kernel(
    s_ref, up_ref, w_ref, bias_ref, proj_ref, w2_ref, bias2_ref, proj2_ref,
    act_ref, slope_ref, mid_ref, pre_ref, pre2_ref, back_ref, w_t_ref, w2_t_ref, proj_t_ref,
):
    at = lambda j: s_ref[j]

    def product(j):
        return dot(taps(at, j, 1), w_ref[...]) + bias_ref[...]

    pre = product(1)
    for j in range(1, 5):
        after = product(j + 1) if j < 4 else None
        cdf = normal_cdf(pre)
        act = (pre * cdf).astype(BF)
        act_ref[j - 1] = act
        slope_ref[j - 1] = slope_of(pre, cdf).astype(BF)
        mid_ref[j - 1] = (s_ref[j].astype(F32) + dot(act, proj_ref[...])).astype(BF)
        pre = after
    pre_ref[0] = dot(s_ref[0], tap(w_ref, 2)) + bias_ref[...]
    pre_ref[1] = dot(s_ref[0], tap(w_ref, 1)) + dot(s_ref[1], tap(w_ref, 2)) + bias_ref[...]
    pre_ref[2] = dot(s_ref[4], tap(w_ref, 0)) + dot(s_ref[5], tap(w_ref, 1)) + bias_ref[...]
    pre_ref[3] = dot(s_ref[5], tap(w_ref, 0)) + bias_ref[...]
    for j in range(6):
        total = bias2_ref[...]
        for k in range(3):
            if 1 <= j + 2 * (k - 1) <= 4:
                total = total + dot(mid_ref[j + 2 * (k - 1) - 1], tap(w2_ref, k))
        pre2_ref[j] = total
    for k in range(3):
        to = slice((2 - k) * C, (3 - k) * C)
        w_t_ref[to] = tap(w_ref, k).T
        w2_t_ref[to] = tap(w2_ref, k).T
    proj_t_ref[...] = proj_ref[...].T
    proj2_t = proj2_ref[...].T
    for j in range(6):
        back_ref[j] = dot(up_ref[j], proj2_t)


def pair(one, two):
    return jnp.concatenate([one, two], axis=1)


def far_kernel(
    s_ref, one_ref, two_ref, near_ref, pre_ref, pre2_ref, back_ref, w_ref, proj_ref, w2_ref,
    mid_ref, act2_ref, delta_ref, halo_ref, to_one_ref, to_two_ref,
):
    turned = odd() == 1
    for k in range(2):
        one, two = one_ref[k], two_ref[k]
        halo_ref[k] = jnp.where(turned, two, one)
        halo_ref[2 + k] = jnp.where(turned, one, two)

    def at(j):
        return halo_ref[j + 2] if j < 0 else halo_ref[j - 4] if j > 5 else s_ref[j]

    def product(j):
        if j == -1:
            return pre_ref[0] + dot(pair(at(-2), at(-1)), w_ref[: 2 * C])
        return pre_ref[3] + dot(pair(at(6), at(7)), w_ref[C:])

    def product2(i):
        if i == 0:
            return pre2_ref[1] + dot(mid_ref[0], tap(w2_ref, 0))
        return pre2_ref[4] + dot(mid_ref[1], tap(w2_ref, 2))

    order = (-1, 6)
    pre = product(order[0])
    for n, j in enumerate(order):
        after = product(order[n + 1]) if n < 1 else product2(0)
        act = (pre * normal_cdf(pre)).astype(BF)
        mid_ref[n] = (at(j).astype(F32) + dot(act, proj_ref[...])).astype(BF)
        pre = after
    for i, j in enumerate((1, 4)):
        after = product2(1) if i == 0 else None
        cdf = normal_cdf(pre)
        act2_ref[i] = (pre * cdf).astype(BF)
        delta_ref[i] = (back_ref[j] * slope_of(pre, cdf)).astype(BF)
        pre = after
    to_one_ref[0] = jnp.where(turned, delta_ref[1], delta_ref[0])
    to_two_ref[0] = jnp.where(turned, delta_ref[0], delta_ref[1])


def mids_kernel(s_ref, halo_ref, pre_ref, w_ref, proj_ref, act_ref, slope_ref, mid_ref):
    pres = [
        pre_ref[1] + dot(halo_ref[1], tap(w_ref, 0)),
        pre_ref[2] + dot(halo_ref[2], tap(w_ref, 2)),
    ]
    for i, pre in enumerate(pres):
        cdf = normal_cdf(pre)
        act = (pre * cdf).astype(BF)
        act_ref[i] = act
        slope_ref[i] = slope_of(pre, cdf).astype(BF)
        mid_ref[i] = (s_ref[5 * i].astype(F32) + dot(act, proj_ref[...])).astype(BF)


def last_kernel(
    halo_ref, one_ref, two_ref, near_mid_ref, pre2_ref, back_ref, w_ref, bias_ref, proj_ref, w2_ref,
    mid_ref, act2_ref, delta_ref, to_one_ref, to_two_ref,
):
    turned = odd() == 1
    low = jnp.where(turned, two_ref[0], one_ref[0])
    high = jnp.where(turned, one_ref[0], two_ref[0])
    three = (
        jnp.concatenate([low, halo_ref[0], halo_ref[1]], axis=1),
        jnp.concatenate([halo_ref[2], halo_ref[3], high], axis=1),
    )

    def product2(i):
        if i == 0:
            return pre2_ref[0] + dot(pair(mid_ref[0], near_mid_ref[0]), w2_ref[: 2 * C])
        return pre2_ref[5] + dot(pair(near_mid_ref[1], mid_ref[1]), w2_ref[C:])

    pre = dot(three[0], w_ref[...]) + bias_ref[...]
    for i in range(2):
        after = dot(three[1], w_ref[...]) + bias_ref[...] if i == 0 else product2(0)
        act = (pre * normal_cdf(pre)).astype(BF)
        mid_ref[i] = (halo_ref[3 * i].astype(F32) + dot(act, proj_ref[...])).astype(BF)
        pre = after
    for i, j in enumerate((0, 5)):
        after = product2(1) if i == 0 else None
        cdf = normal_cdf(pre)
        act2_ref[i] = (pre * cdf).astype(BF)
        delta_ref[i] = (back_ref[j] * slope_of(pre, cdf)).astype(BF)
        pre = after
    to_one_ref[0] = jnp.where(turned, delta_ref[1], delta_ref[0])
    to_two_ref[0] = jnp.where(turned, delta_ref[0], delta_ref[1])


def add_grads(sum_ref, base_ref, cells, delta, act, up):
    conv = t_dot(cells, delta)
    proj = t_dot(act, up)
    sum_ref[: 3 * C] = conv if base_ref is None else base_ref[: 3 * C] + conv
    sum_ref[3 * C :] = proj if base_ref is None else base_ref[3 * C :] + proj
    return jnp.sum(delta.astype(F32), axis=0, keepdims=True)


def put_halves(sum_ref, bias, row, away_ref, mine_ref):
    core = lax.axis_index("core")
    half = 2 * C
    mine_ref[:half] = sum_ref[pl.ds(pl.multiple_of(core * half, half), half)].astype(BF)
    away_ref[:half] = sum_ref[pl.ds(pl.multiple_of((1 - core) * half, half), half)].astype(BF)
    at = lax.broadcasted_iota(jnp.int32, (16, C), 0)
    tail = jnp.where(at == row, jnp.broadcast_to(bias, (16, C)), 0.0).astype(BF)
    mine_ref[half:] = tail
    away_ref[half:] = tail


def inner_kernel(
    near_ref, far_ref, mids_ref, last_ref, act2_far_ref, act2_last_ref, up_ref, delta_far_ref, delta_last_ref,
    pre2_ref, back_ref, w2_ref, w_t_ref, proj_t_ref, slope_ref, s_ref, act_ref,
    away_ref, mine_ref, below_ref, grad_ref, out_ref, sum_ref, bias_ref, total_ref,
):
    def mid_at(j):
        if j in (-2, 7):
            return last_ref[0 if j < 0 else 1]
        if j in (-1, 6):
            return far_ref[0 if j < 0 else 1]
        return mids_ref[j // 5] if j in (0, 5) else near_ref[j - 1]

    at = lambda j: s_ref[j]
    delta = {1: delta_far_ref[0], 4: delta_far_ref[1], 0: delta_last_ref[0], 5: delta_last_ref[1]}
    act2 = {1: act2_far_ref[0], 4: act2_far_ref[1], 0: act2_last_ref[0], 5: act2_last_ref[1]}
    products = {
        2: pre2_ref[2] + dot(mid_at(0), tap(w2_ref, 0)),
        3: pre2_ref[3] + dot(mid_at(5), tap(w2_ref, 2)),
    }
    bias = jnp.zeros((1, C), F32)
    for n, j in enumerate((0, 5, 1, 4, 2, 3)):
        if n in (1, 2):
            i = n + 1
            pre = products[i]
            cdf = normal_cdf(pre)
            act2[i] = (pre * cdf).astype(BF)
            delta[i] = (back_ref[i] * slope_of(pre, cdf)).astype(BF)
        bias += add_grads(total_ref, total_ref if n else None, taps(mid_at, j, 2), delta[j], act2[j], up_ref[j])
    put_halves(total_ref, bias, 0, away_ref, mine_ref)
    for i, j in enumerate((0, 1, 4, 5)):
        low = slice(C, 3 * C) if j < 2 else slice(0, 2 * C)
        two = pair(delta[j], delta[j + 2]) if j < 2 else pair(delta[j - 2], delta[j])
        below_ref[i] = up_ref[j].astype(F32) + dot(two, w_t_ref[low])
    bias = jnp.zeros((1, C), F32)
    for j in (2, 3):
        three = jnp.concatenate([delta[j - 2], delta[j], delta[j + 2]], axis=1)
        below = (up_ref[j].astype(F32) + dot(three, w_t_ref[...])).astype(BF)
        grad_ref[j - 2] = below
        first = (dot(below, proj_t_ref[...]) * slope_ref[j - 1].astype(F32)).astype(BF)
        out_ref[j - 2] = first
        bias += add_grads(sum_ref, sum_ref if j > 2 else None, taps(at, j, 1), first, act_ref[j - 1], below)
    bias_ref[...] = bias


def ends_kernel(
    below_ref, one_ref, two_ref, w_t_ref, proj_t_ref, slope_ref, s_ref, halo_ref, act_ref, part_ref, part_bias_ref,
    grad_ref, out_ref, to_one_ref, to_two_ref, sum_ref, bias_ref,
):
    turned = odd() == 1

    def at(j):
        return halo_ref[1] if j < 0 else halo_ref[2] if j > 5 else s_ref[j]

    def product(i):
        if i == 0:
            far = dot(jnp.where(turned, two_ref[0], one_ref[0]), tap(w_t_ref, 0))
        else:
            far = dot(jnp.where(turned, one_ref[0], two_ref[0]), tap(w_t_ref, 2))
        return (below_ref[3 * i] + far).astype(BF)

    bias = part_bias_ref[...]
    below = [product(0), product(1)]
    for i, j in enumerate((0, 5)):
        grad_ref[i] = below[i]
        delta = (dot(below[i], proj_t_ref[...]) * slope_ref[i].astype(F32)).astype(BF)
        out_ref[i] = delta
        bias += add_grads(sum_ref, sum_ref if i else part_ref, taps(at, j, 1), delta, act_ref[i], below[i])
    bias_ref[...] = bias
    to_one_ref[0] = jnp.where(turned, out_ref[1], out_ref[0])
    to_two_ref[0] = jnp.where(turned, out_ref[0], out_ref[1])


def edge_kernel(
    below_ref, one_ref, two_ref, w_t_ref, proj_t_ref, slope_ref, s_ref, act_ref, part_ref, part_bias_ref,
    grad_ref, out_ref, away_ref, mine_ref, sum_ref,
):
    at = lambda j: s_ref[j]
    turned = odd() == 1

    def product(i):
        if i == 0:
            far = dot(jnp.where(turned, two_ref[0], one_ref[0]), tap(w_t_ref, 0))
        else:
            far = dot(jnp.where(turned, one_ref[0], two_ref[0]), tap(w_t_ref, 2))
        return (below_ref[1 + i] + far).astype(BF)

    bias = part_bias_ref[...]
    below = [product(0), product(1)]
    for i, j in enumerate((1, 4)):
        grad_ref[i] = below[i]
        delta = (dot(below[i], proj_t_ref[...]) * slope_ref[j - 1].astype(F32)).astype(BF)
        out_ref[i] = delta
        base_ref = sum_ref if i else part_ref
        bias += add_grads(sum_ref, base_ref, taps(at, j, 1), delta, act_ref[j - 1], below[i])
    put_halves(sum_ref, bias, 1, away_ref, mine_ref)


def pair_kernel(mine_b_ref, near_b_ref, mine_a_ref, near_a_ref, done_ref, out_ref):
    n, rows, _ = out_ref.shape
    chunk = (rows - 16) // 2

    def both(mine, near, part):
        return mine[part].astype(F32) + near[part].astype(F32)

    last = slice(n * chunk, n * chunk + 16)
    tail = (both(mine_b_ref, near_b_ref, last) + both(mine_a_ref, near_a_ref, last)).astype(BF)
    for i in range(n):
        part = slice(i * chunk, (i + 1) * chunk)
        out_ref[i, :chunk] = both(mine_b_ref, near_b_ref, part).astype(BF)
        out_ref[i, chunk : 2 * chunk] = both(mine_a_ref, near_a_ref, part).astype(BF)
        out_ref[i, 2 * chunk :] = tail


def rest_kernel(got_ref, out_ref):
    total = got_ref[0].astype(F32)
    for i in range(1, got_ref.shape[0]):
        total += got_ref[i].astype(F32)
    total = total.astype(BF)
    for i in range(out_ref.shape[0]):
        out_ref[i] = total


def token_kernel(one_ref, two_ref, out_ref):
    out_ref[...] = jnp.zeros(out_ref.shape, F32)


def ring_kernel(got_ref, token_ref, out_ref, bias_b_ref, bias_a_ref):
    total = got_ref[0].astype(F32) + token_ref[0:1, 0:1]
    for i in range(1, got_ref.shape[0]):
        total += got_ref[i].astype(F32)
    chunk = out_ref.shape[1]
    own = total[:chunk].astype(BF)
    for i in range(out_ref.shape[0]):
        out_ref[i] = own
    bias_b_ref[...] = total[chunk : chunk + 1]
    bias_a_ref[...] = total[chunk + 1 : chunk + 2]


def tail_kernel(mine_ref, other_ref, conv_b_ref, proj_b_ref, conv_a_ref, proj_a_ref, work, sems):
    core = lax.axis_index("core")
    n, rows, _ = mine_ref.shape
    chunk = rows // 2

    def put(low, high):
        copies = []
        for at in range(8):
            src, matrix, part = (low, high)[at // 4], at // 2 % 2, at % 2
            conv, proj = ((conv_b_ref, proj_b_ref), (conv_a_ref, proj_a_ref))[part]
            for i in range(n // 2):
                to, of = slice(i * chunk, (i + 1) * chunk), slice(part * chunk, (part + 1) * chunk)
                work[at, to] = src[matrix * (n // 2) + i, of].astype(F32)
            to = conv.at[matrix] if at < 4 else conv.at[2] if matrix == 0 else proj
            copies.append(pltpu.make_async_copy(work.at[at], to, sems.at[at]))
            copies[at].start()
        for copy in copies:
            copy.wait()

    @pl.when(core == 0)
    def _():
        put(mine_ref, other_ref)

    @pl.when(core != 0)
    def _():
        put(other_ref, mine_ref)


def lower_inner_kernel(
    inner_ref, ends_ref, edge_ref, in_up_ref, ends_up_ref, edge_up_ref, w_ref, out_ref, part_ref
):
    def place(j, inner, ends, edge):
        return inner[j - 2] if j in (2, 3) else ends[j // 5] if j in (0, 5) else edge[j // 4]

    at = lambda j: place(j, inner_ref, ends_ref, edge_ref)
    for j in range(1, 5):
        up = place(j, in_up_ref, ends_up_ref, edge_up_ref)
        out_ref[j - 1] = (up.astype(F32) + dot(taps(at, j, 1), w_ref[...])).astype(BF)
    for i, own, low in ((0, (0, 1), C), (1, (4, 5), 0)):
        two = pair(at(own[0]), at(own[1]))
        part_ref[i] = ends_up_ref[i].astype(F32) + dot(two, w_ref[low : low + 2 * C])


def lower_outer_kernel(part_ref, w_ref, one_ref, two_ref, inner_ref, out_ref, parts, ends, sems):
    copies = [
        pltpu.make_async_copy(one_ref, parts.at[pl.ds(odd(), 1)], sems.at[0]),
        pltpu.make_async_copy(two_ref, parts.at[pl.ds(1 - odd(), 1)], sems.at[1]),
        pltpu.make_async_copy(inner_ref, out_ref.at[pl.ds(1, 4)], sems.at[2]),
    ]
    for copy in copies:
        copy.start()
    copies[0].wait()
    copies[1].wait()
    last = []
    for i in range(2):
        ends[i] = (part_ref[i] + dot(parts[i], tap(w_ref, 2 * i))).astype(BF)
        last.append(pltpu.make_async_copy(ends.at[pl.ds(i, 1)], out_ref.at[pl.ds(5 * i, 1)], sems.at[3 + i]))
        last[i].start()
    for copy in last + copies[2:]:
        copy.wait()


def call(kernel, outs, args, flops=0, scratch=(), far=0, far_out=False):
    vmem, hbm = pl.BlockSpec(memory_space=pltpu.VMEM), pl.BlockSpec(memory_space=pltpu.HBM)
    moved = flops if flops == 1024 else sum(a.size * a.dtype.itemsize for a in args) + sum(
        math.prod(s) * jnp.dtype(t).itemsize for s, t in outs
    )
    return pl.pallas_call(
        kernel,
        out_shape=[jax.ShapeDtypeStruct(s, t) for s, t in outs],
        in_specs=[vmem] * (len(args) - far) + [hbm] * far,
        out_specs=[hbm if far_out else vmem] * len(outs),
        scratch_shapes=list(scratch),
        compiler_params=pltpu.CompilerParams(vmem_limit_bytes=32 * 2**20),
        cost_estimate=pl.CostEstimate(flops=flops, bytes_accessed=moved, transcendentals=0),
        name=kernel.__name__[: -len("_kernel")],
    )(*args)


def exchange(to_one, to_two):
    n = lax.axis_size(RING)
    one = [(i, (i + 1 if i % 2 else i - 1) % n) for i in range(n)]
    two = [(i, (i - 1 if i % 2 else i + 1) % n) for i in range(n)]
    return lax.ppermute(to_one, RING, one), lax.ppermute(to_two, RING, two)


def across(cells):
    return lax.ppermute(cells, "core", [(0, 1), (1, 0)])


def on_device(signals, cotangent, kernel_a, bias_a, proj_a, kernel_b, bias_b, proj_b):
    batch, length, channels = signals.shape
    unit = 2 * BLOCK * C * C
    cells = signals.reshape(-1, BLOCK, C)
    up = cotangent.reshape(-1, BLOCK, C)
    rest, ring = lax.axis_size(PLANE), lax.axis_size(COLUMN)
    wa, wb = kernel_a.reshape(3 * C, C), kernel_b.reshape(3 * C, C)
    ba, bb = bias_a.reshape(1, C), bias_b.reshape(1, C)

    def like(n, t=BF):
        return ((n, BLOCK, C), t)

    to_one, to_two, to_one_far, to_two_far = call(
        cut_kernel,
        [like(2), like(2), like(1), like(1)],
        [cells],
        scratch=[pltpu.SemaphoreType.DMA((4,))],
        far=1,
    )
    s_one, s_two = exchange(to_one, to_two)
    s_one_far, s_two_far = exchange(to_one_far, to_two_far)
    act_near, slope_near, mid_near, pre_a, pre_b, back, wa_t, wb_t, pa_t = call(
        near_kernel,
        [like(4)] * 3 + [like(4, F32), like(6, F32), like(6, F32)] + [((3 * C, C), BF)] * 2 + [((C, C), BF)],
        [cells, up, wa, ba, proj_a, wb, bb, proj_b],
        1024,
    )
    mid_far, act_b_far, delta_b_far, halo, to_one, to_two = call(
        far_kernel,
        [like(2), like(2), like(2), like(4), like(1), like(1)],
        [cells, s_one, s_two, mid_near, pre_a, pre_b, back, wa, proj_a, wb],
        1024,
    )
    d_one, d_two = exchange(to_one, to_two)
    act_far, slope_far, mids = call(
        mids_kernel, [like(2)] * 3, [cells, halo, pre_a, wa, proj_a], 1024
    )
    mid_last, act_b_last, delta_b_last, to_one, to_two = call(
        last_kernel,
        [like(2), like(2), like(2), like(1), like(1)],
        [halo, s_one_far, s_two_far, mids, pre_b, back, wa, ba, proj_a, wb],
        1024,
    )
    d_one_far, d_two_far = exchange(to_one, to_two)
    half = ((2 * C + 16, C), BF)
    away_b, mine_b, below, grad_in, delta_in, part, part_bias = call(
        inner_kernel,
        [half, half, like(4, F32), like(2), like(2), ((4 * C, C), F32), ((1, C), F32)],
        [mid_near, mid_far, mids, mid_last, act_b_far, act_b_last, up, delta_b_far, delta_b_last]
        + [pre_b, back, wb, wb_t, pa_t, slope_near, cells, act_near],
        1024,
        [pltpu.VMEM((4 * C, C), F32)],
    )
    grad_end, delta_end, to_one, to_two, part, part_bias = call(
        ends_kernel,
        [like(2), like(2), like(1), like(1), ((4 * C, C), F32), ((1, C), F32)],
        [below, d_one, d_two, wb_t, pa_t, slope_far, cells, halo, act_far, part, part_bias],
        1024,
    )
    e_one, e_two = exchange(to_one, to_two)
    near_b = across(away_b)
    grad_out, delta_out, away_a, mine_a = call(
        edge_kernel,
        [like(2), like(2), half, half],
        [below, d_one_far, d_two_far, wb_t, pa_t, slope_near, cells, act_near, part, part_bias],
        12 * unit,
        [pltpu.VMEM((4 * C, C), F32)],
    )
    inside, outside = call(
        lower_inner_kernel,
        [like(4), like(2, F32)],
        [delta_in, delta_end, delta_out, grad_in, grad_end, grad_out, wa_t],
        16 * unit,
    )
    chunk = 2 * C // rest
    (sent,) = call(
        pair_kernel,
        [((rest, 2 * chunk + 16, C), BF)],
        [mine_b, near_b, mine_a, across(away_a), inside],
        far=1,
    )
    got = lax.all_to_all(sent, PLANE, 0, 0)
    (sent,) = call(rest_kernel, [((ring, 2 * chunk + 16, C), BF)], [got])
    got = lax.all_to_all(sent, COLUMN, 0, 0)
    (token,) = call(token_kernel, [((8, 128), F32)], [e_one, e_two], far=2)
    sent, sum_bias_b, sum_bias_a = call(
        ring_kernel, [((rest, 2 * chunk, C), BF), ((1, C), F32), ((1, C), F32)], [got, token]
    )
    mine = lax.all_to_all(sent, PLANE, 0, 0)
    conv_b, grad_proj_b, conv_a, grad_proj_a = call(
        tail_kernel,
        [((3, C, C), F32), ((C, C), F32)] * 2,
        [mine, across(mine)],
        scratch=[pltpu.VMEM((8, C, C), F32), pltpu.SemaphoreType.DMA((8,))],
        far_out=True,
    )
    (out,) = call(
        lower_outer_kernel,
        [like(6)],
        [outside, wa_t, e_one, e_two, inside],
        2 * unit,
        [pltpu.VMEM((2, BLOCK, C), BF)] * 2 + [pltpu.SemaphoreType.DMA((5,))],
        far=3,
        far_out=True,
    )
    return (
        out.reshape(batch, length, channels),
        conv_a,
        sum_bias_a.reshape(C),
        grad_proj_a,
        conv_b,
        sum_bias_b.reshape(C),
        grad_proj_b,
    )


def solution(mesh):
    split = Mesh(mesh.devices.reshape(2, 4, 8, 2, 2), ("xh", "y", "z", "xl", "core"))
    data = P(("z", "xl", "core"), RING, None)
    return jax.shard_map(
        on_device,
        mesh=split,
        in_specs=(data, data, P(), P(), P(), P(), P(), P()),
        out_specs=(data, P(), P(), P(), P(), P(), P()),
        check_vma=False,
    )
```
